32 devices in a mesh: grp: 2 (over y), chan: 8 (over z, core), bl: 2 (over x).
Axes of the slice: x: 2, y: 2, z: 4, core: 2. Of those that a mesh axis runs over, the one named last changes fastest.
Arguments:
- patches: bfloat16 [32, 2, 2, 64, 8192], P(None, None, None, ('grp', 'chan'), 'bl'), parts along dimension 3, may hold values from -1.5 to 1.5
- visibilities: float32 [2, 2, 64, 8192], P(None, None, ('grp', 'chan'), 'bl'), parts along dimension 2, may hold values from -6 to 6
- valid: int32 [64, 8192], P(('grp', 'chan'), 'bl'), parts along dimension 0, may hold values 0 or 1
- baseline_stations: int32 [2, 8192], P(None, 'bl'), may hold values from 0 to 511, as said below
- cluster: int32 [32, 1], replicated, may hold values from 0 to 15
- gains: float32 [2, 16, 64, 512], P(None, None, ('grp', 'chan'), 'bl'), parts along dimension 2, may hold values from -1 to 1
Outputs:
- new_gains: float32 [2, 16, 64, 512], P(None, None, ('grp', 'chan'), 'bl'), parts along dimension 2
The draws below stay inside these ranges and needn't reach their ends.
There are 2 independent parts, one for each index of `grp`. The reference program is written for one: setup_inputs(seed, part) draws one part's arguments, and reference() takes and returns one part's arrays. A program takes and returns all parts, laid end to end along the dimension named above; an argument that names none is the same for every part. Nothing has to cross between parts.
Inputs may be any that keep to these rules, and one draw needn't show every extreme that they name: `baseline_stations`: row 0 holds each baseline's lower station and row 1 its higher one; the two always differ. `cluster`: every direction has at least one patch.
All inputs are finite; a program needn't handle non-finite values. No bound on the sum of `valid` on one device may be relied on, other than what follows from the above.
Results may differ from the reference program's by a relative error of at most 0.0015.
Values may be sent and summed in bfloat16 or wider, within the bound.
No kernel may reach another device: no remote copies, remote signals or barrier semaphores. Data moves between devices by JAX's collectives and lax.ppermute only.
A program may use at most 64 MiB of HBM per device.

```python
import jax
import jax.numpy as jnp
from jax import lax

STATION_COUNT = 512
DIRECTIONS = 16
SKY_PATCHES = 32
TIME_SLOTS = 2
ITERS = 2
WINDOW_CHANNELS = 32
BASELINE_COUNT = 8192


def draw_baseline_stations(key, part):
    key = jax.random.fold_in(key, 11)
    leading_key, shifted_key = jax.random.split(key)
    leading = jax.random.randint(leading_key, (BASELINE_COUNT,), 0, STATION_COUNT, dtype=jnp.int32)
    shift_amount = jax.random.randint(shifted_key, (BASELINE_COUNT,), 1, STATION_COUNT, dtype=jnp.int32)
    second = (leading + shift_amount) % STATION_COUNT
    lower = jnp.minimum(leading, second).at[0].set(0)
    higher = jnp.maximum(leading, second).at[0].set(STATION_COUNT - 1)
    return jnp.stack([lower, higher]).astype(jnp.int32)


def plant(result, rng, smallest, top_value):
    longest = result.shape.index(max(result.shape))
    spots = []
    for shift in (0, 1):
        where = [jax.random.randint(jax.random.fold_in(rng, axis), (), 0, length) for axis, length in enumerate(result.shape)]
        where[longest] = (where[longest] + shift) % result.shape[longest]
        spots.append(tuple(where))
    return result.at[spots[0]].set(smallest).at[spots[1]].set(top_value)


def shard_levels(own_key, dims, shards, least, top_value):
    level, own = 1.0, jax.random.fold_in(own_key, 6)
    for position, blocks in shards:
        steps = jnp.exp(jax.random.uniform(jax.random.fold_in(own, position), (blocks,), jnp.float32, least / len(shards), top_value / len(shards)))
        level = level * jnp.repeat(steps, dims[position] // blocks).reshape([-1 if axis == position else 1 for axis in range(len(dims))])
    return level


def distinct(rng, rows, amount, top, lift):
    order = jax.random.permutation(jax.random.fold_in(rng, 1), amount)
    pull = order
    for power in range(3):
        pull = pull * pull // amount
    pull = pull * lift // amount
    lots = jax.random.randint(jax.random.fold_in(rng, 2), (rows, amount), 0, 4096) + pull
    fixed_rows = jax.random.permutation(jax.random.fold_in(rng, 3), rows)[jnp.arange(amount) % rows]
    lots = jnp.where(jnp.arange(rows)[:, None] == fixed_rows[None, :], 1 << 14, lots)
    merit = lots * amount + jnp.arange(amount)
    return lax.top_k(merit.astype(jnp.int32), top)[1].astype(jnp.int32)


def centred(own_key, extent, scale, most, cuts=(), kind=jnp.bfloat16):
    loudness = shard_levels(own_key, extent, cuts, -0.22, 0.18) if cuts else 1.0
    entries = jax.random.normal(own_key, extent, jnp.float32) * scale * loudness
    return jnp.minimum(jnp.maximum(entries, -most), most).astype(kind)


def setup_inputs(seed: int = 0, part: int = 0) -> dict:
    arg_keys = jax.random.split(jax.random.key(seed), 7)
    own_keys = jax.random.split(jax.random.fold_in(arg_keys[6], part), 7)
    patches = centred(own_keys[0], (SKY_PATCHES, 2, TIME_SLOTS, WINDOW_CHANNELS, BASELINE_COUNT), 0.25, 1.5, ((3, 8), (4, 2)))
    visibilities = centred(own_keys[1], (2, TIME_SLOTS, WINDOW_CHANNELS, BASELINE_COUNT), 1.0, 6.0, ((2, 8), (3, 2)), jnp.float32)
    valid = plant((jax.random.randint(own_keys[2], (WINDOW_CHANNELS, BASELINE_COUNT), 0, 8) < 7).astype(jnp.int32), jax.random.fold_in(own_keys[2], 1), 0, 1)
    baseline_stations = draw_baseline_stations(jax.random.fold_in(arg_keys[6], 71), part)
    cluster = distinct(arg_keys[4], SKY_PATCHES, DIRECTIONS, 1, 0)
    gains = jnp.clip(jax.random.uniform(own_keys[5], (2, DIRECTIONS, WINDOW_CHANNELS, STATION_COUNT), jnp.float32, -1.0, 1.0) * shard_levels(own_keys[5], (2, DIRECTIONS, WINDOW_CHANNELS, STATION_COUNT), ((2, 8), (3, 2)), -0.4, 0.0), -1.0, 1.0)
    return dict(patches=patches, visibilities=visibilities, valid=valid, baseline_stations=baseline_stations, cluster=cluster, gains=gains)


def make_basis(channel, total):
    ratio = 1.0 + channel / total
    inverse = 4.0 / ratio - 3.0
    return jnp.stack([jnp.ones_like(inverse), inverse, 2.0 * inverse * inverse - 1.0])

def basis_products(basis):
    return jnp.stack([basis[0] * basis[0], basis[0] * basis[1], basis[0] * basis[2], basis[1] * basis[1], basis[1] * basis[2], basis[2] * basis[2]])

def normal_terms(updated, weight, basis):
    highest = lax.Precision.HIGHEST
    normal_matrix = jnp.einsum('jc,kcs->jks', basis_products(basis), weight, precision=highest)
    right = jnp.einsum('bc,xkcs->xbks', basis, weight[None] * updated, precision=highest)
    return (normal_matrix, right)

def solve_three(normal_matrix, right):
    low_aa = jnp.sqrt(normal_matrix[0])
    low_ba = normal_matrix[1] / low_aa
    low_ca = normal_matrix[2] / low_aa
    low_bb = jnp.sqrt(normal_matrix[3] - low_ba * low_ba)
    low_cb = (normal_matrix[4] - low_ca * low_ba) / low_bb
    low_cc = jnp.sqrt(normal_matrix[5] - low_ca * low_ca - low_cb * low_cb)
    first_y = right[:, 0] / low_aa
    second_y = (right[:, 1] - low_ba * first_y) / low_bb
    third_y = (right[:, 2] - low_ca * first_y - low_cb * second_y) / low_cc
    third_x = third_y / low_cc
    second_x = (second_y - low_cb * third_x) / low_bb
    first_x = (first_y - low_ba * second_x - low_ca * third_x) / low_aa
    return jnp.stack([first_x, second_x, third_x], axis=1)

def evaluate(coefs, basis):
    return jnp.einsum('xbks,bc->xkcs', coefs, basis, precision=lax.Precision.HIGHEST)

def baseline_terms(model, visible, validity, leading, second):
    model_re = model[:, 0]
    model_im = model[:, 1]
    first_re = leading[0][:, None]
    first_im = leading[1][:, None]
    second_re = second[0][:, None]
    second_im = second[1][:, None]
    far_re = model_re * second_re + model_im * second_im
    far_im = model_im * second_re - model_re * second_im
    pred_re = lax.optimization_barrier(jnp.sum(first_re * far_re - first_im * far_im, axis=0))
    pred_im = lax.optimization_barrier(jnp.sum(first_re * far_im + first_im * far_re, axis=0))
    resid_re = visible[0] - pred_re
    resid_im = visible[1] - pred_im
    near_re = model_re * first_re - model_im * first_im
    near_im = model_re * first_im + model_im * first_re
    upper = jnp.stack([lax.optimization_barrier(jnp.sum(validity * (far_re * resid_re + far_im * resid_im), axis=1)), lax.optimization_barrier(jnp.sum(validity * (far_re * resid_im - far_im * resid_re), axis=1)), lax.optimization_barrier(jnp.sum(validity * (far_re * far_re + far_im * far_im), axis=1))])
    lower = jnp.stack([lax.optimization_barrier(jnp.sum(validity * (near_re * resid_re + near_im * resid_im), axis=1)), lax.optimization_barrier(jnp.sum(validity * (near_im * resid_re - near_re * resid_im), axis=1)), lax.optimization_barrier(jnp.sum(validity * (near_re * near_re + near_im * near_im), axis=1))])
    return (upper.astype(jnp.bfloat16), lower.astype(jnp.bfloat16))

def channel_sums(patch, visible, validity, gain, onehot, first_station, second_station, both_stations):
    model = jnp.dot(onehot, patch.reshape(SKY_PATCHES, -1), preferred_element_type=jnp.float32)
    model = model.reshape(DIRECTIONS, 2, TIME_SLOTS, -1)
    rounded = lax.optimization_barrier(gain.astype(jnp.bfloat16)).astype(jnp.float32)
    leading = rounded[:, :, first_station]
    second = rounded[:, :, second_station]
    upper, lower = baseline_terms(model, visible, validity, leading, second)
    joined = lax.optimization_barrier(jnp.concatenate([upper, lower], axis=2)).astype(jnp.float32)
    summed = jax.ops.segment_sum(joined.reshape(3 * DIRECTIONS, -1).T, both_stations, num_segments=STATION_COUNT)
    return summed.T.reshape(3, DIRECTIONS, STATION_COUNT)

def reference(patches, visibilities, valid, baseline_stations, cluster, gains):
    onehot = (cluster[:, 0][None, :] == jnp.arange(DIRECTIONS, dtype=jnp.int32)[:, None]).astype(jnp.bfloat16)
    first_station = baseline_stations[0]
    second_station = baseline_stations[1]
    both_stations = jnp.concatenate([first_station, second_station])
    validity = valid.astype(jnp.float32)
    basis = make_basis(jnp.arange(WINDOW_CHANNELS, dtype=jnp.float32), WINDOW_CHANNELS)
    current = gains
    for sweep in range(ITERS):

        def one_channel(channel, current=current):
            return channel_sums(lax.dynamic_index_in_dim(patches, channel, 3, False), lax.dynamic_index_in_dim(visibilities, channel, 2, False), lax.dynamic_index_in_dim(validity, channel, 0, False), lax.dynamic_index_in_dim(current, channel, 2, False), onehot, first_station, second_station, both_stations)
        sums = lax.map(one_channel, jnp.arange(WINDOW_CHANNELS, dtype=jnp.int32)).transpose(1, 2, 0, 3)
        weight = sums[2] + 1.0
        updated = current + sums[0:2] / weight
        normal_matrix, right = normal_terms(updated, weight, basis)
        fitted = evaluate(solve_three(normal_matrix, right), basis)
        current = 0.5 * (current + fitted)
    return current
```

```python
from functools import partial

import jax
import jax.numpy as jnp
from jax import lax
from jax.experimental import pallas as pl
from jax.experimental.pallas import tpu as pltpu
from jax.sharding import PartitionSpec as P

DIRECTIONS = 16
SKY_PATCHES = 32
TIME_SLOTS = 2
ITERS = 2
LANES = 128
PREP_CHUNK = 1024
SWEEP_CHUNK = 1024
HALF = DIRECTIONS // 2
HIGHEST = lax.Precision.HIGHEST
F32, BF16 = jnp.float32, jnp.bfloat16


def basis_at(channel, total):
    ratio = 1.0 + channel.astype(F32) / total
    inverse = 4.0 / ratio - 3.0
    return jnp.ones_like(inverse), inverse, 2.0 * inverse * inverse - 1.0


def iotas(shape):
    return lax.broadcasted_iota(jnp.int32, shape, 0), lax.broadcasted_iota(jnp.int32, shape, 1)


def pick(index, values):
    out = values[-1]
    for k in range(len(values) - 2, -1, -1):
        out = jnp.where(index == k, values[k], out)
    return out


def moment_matrix(terms, channels, total, chan):
    row, col = iotas((2 * terms * HALF, DIRECTIONS * channels))
    block = row // HALF
    half = (block >= terms).astype(jnp.int32)
    term = block - half * terms
    direction = jnp.bitwise_xor(half, lax.rem(chan, 2)) * HALF + row % HALF
    one, first, second = basis_at(chan * channels + col % channels, total)
    if terms == 6:
        values = (one, first, second, first * first, first * second, second * second)
    else:
        values = (one, first, second)
    return jnp.where(direction == col // channels, pick(term, values), 0.0)


def fit_matrix(half, channels, total, chan):
    per = DIRECTIONS * channels
    row, col = iotas((2 * per, 6 * HALF))
    place = row % per
    block = col // HALF
    direction = jnp.bitwise_xor(half, lax.rem(chan, 2)) * HALF + col % HALF
    basis = basis_at(chan * channels + place % channels, total)
    same = (direction == place // channels) & (row // per == block // 3)
    return jnp.where(same, pick(block % 3, basis), 0.0)


def prep_kernel(total, channels, cluster_ref, patches_ref, valid_ref, model_ref, power_ref,
                normal_ref, right_ref, fit_ref, order_ref, start_ref):
    chan = lax.axis_index("chan")

    @pl.when(pl.program_id(0) == 0)
    def _():
        for d in range(DIRECTIONS + 1):
            start_ref[d] = 0

        @pl.loop(0, SKY_PATCHES)
        def _(q):
            d = cluster_ref[q]
            start_ref[d + 1] = start_ref[d + 1] + 1

        for d in range(DIRECTIONS):
            start_ref[d + 1] = start_ref[d + 1] + start_ref[d]
        for d in range(DIRECTIONS):
            start_ref[DIRECTIONS + 1 + d] = start_ref[d]

        @pl.loop(0, SKY_PATCHES)
        def _(q):
            d = cluster_ref[q]
            place = start_ref[DIRECTIONS + 1 + d]
            order_ref[place] = q
            start_ref[DIRECTIONS + 1 + d] = place + 1

        normal_ref[...] = moment_matrix(6, channels, total, chan)
        right_ref[...] = moment_matrix(3, channels, total, chan)
        fit_ref[0] = fit_matrix(0, channels, total, chan)
        fit_ref[1] = fit_matrix(1, channels, total, chan)

    width = valid_ref.shape[1]
    validity = valid_ref[...].astype(F32)
    parts = [(x, t) for x in range(2) for t in range(TIME_SLOTS)]
    for d in range(DIRECTIONS):

        def add(i, sums):
            q = order_ref[i]
            return tuple(
                s + patches_ref[q, x, t].astype(F32) for s, (x, t) in zip(sums, parts)
            )

        zero = jnp.zeros((channels, width), F32)
        sums = lax.fori_loop(start_ref[d], start_ref[d + 1], add, (zero,) * len(parts))
        power = sums[0] * sums[0]
        for s in sums[1:]:
            power = power + s * s
        rows = slice(d * channels, (d + 1) * channels)
        for s, (x, t) in zip(sums, parts):
            model_ref[x, t, rows, :] = s
        power_ref[rows, :] = power * validity


def prepare(cluster, patches, valid, total):
    channels, baselines = valid.shape
    chunk = min(PREP_CHUNK, baselines)
    per = DIRECTIONS * channels
    whole = lambda shape: pl.BlockSpec(shape, lambda i: (0,) * len(shape))
    return pl.pallas_call(
        partial(prep_kernel, total, channels),
        grid=(baselines // chunk,),
        in_specs=[
            pl.BlockSpec(memory_space=pltpu.SMEM),
            pl.BlockSpec((SKY_PATCHES, 2, TIME_SLOTS, channels, chunk), lambda i: (0, 0, 0, 0, i)),
            pl.BlockSpec((channels, chunk), lambda i: (0, i)),
        ],
        out_specs=[
            pl.BlockSpec((2, TIME_SLOTS, per, chunk), lambda i: (0, 0, 0, i)),
            pl.BlockSpec((per, chunk), lambda i: (0, i)),
            whole((12 * HALF, per)),
            whole((6 * HALF, per)),
            whole((2, 2 * per, 6 * HALF)),
        ],
        out_shape=[
            jax.ShapeDtypeStruct((2, TIME_SLOTS, per, baselines), F32),
            jax.ShapeDtypeStruct((per, baselines), F32),
            jax.ShapeDtypeStruct((12 * HALF, per), F32),
            jax.ShapeDtypeStruct((6 * HALF, per), F32),
            jax.ShapeDtypeStruct((2, 2 * per, 6 * HALF), F32),
        ],
        scratch_shapes=[
            pltpu.SMEM((SKY_PATCHES,), jnp.int32),
            pltpu.SMEM((2 * DIRECTIONS + 1,), jnp.int32),
        ],
        compiler_params=pltpu.CompilerParams(vmem_limit_bytes=32 << 20),
        name="prepare",
    )(cluster, patches, valid)


def fitted_values(fit_ref, coefs):
    out = jnp.dot(fit_ref[0], coefs[0], precision=HIGHEST, preferred_element_type=F32)
    return out + jnp.dot(fit_ref[1], coefs[1], precision=HIGHEST, preferred_element_type=F32)


def sweep_kernel(first, blocks, owned, *refs):
    if first:
        gain_refs, refs = refs[:blocks], refs[blocks:]
    else:
        (before_ref, fit_ref, own_coef_ref, other_coef_ref), refs = refs[:4], refs[4:]
    (stations_ref, model_ref, power_ref, valid_ref, visible_ref, normal_ref, right_ref,
     own_ref, other_ref, current_ref, rounded_ref, sums_ref, near_ref, far_ref,
     upper_ref, lower_ref) = refs
    step = pl.program_id(0)
    channels, width = valid_ref.shape
    per = DIRECTIONS * channels
    stations = blocks * owned

    @pl.when(step == 0)
    def _():
        if first:
            for k in range(blocks):
                for x in range(2):
                    for d in range(DIRECTIONS):
                        row = x * per + d * channels
                        current_ref[row:row + channels, k * owned:(k + 1) * owned] = gain_refs[k][x, d]
        else:
            fitted = fitted_values(fit_ref, (own_coef_ref[...], other_coef_ref[...]))
            current_ref[...] = 0.5 * (before_ref[...] + fitted)
        rounded_ref[...] = current_ref[...].astype(BF16)
        sums_ref[...] = jnp.zeros_like(sums_ref)

    shift = lax.axis_index("bl") * owned
    place = stations_ref[...] - shift
    place = jnp.where(place < 0, place + stations, place)
    ids = lax.broadcasted_iota(jnp.int32, (stations, width), 0)
    first_pick = (ids == place[0:1, :]).astype(BF16)
    second_pick = (ids == place[1:2, :]).astype(BF16)
    rounded = rounded_ref[...]
    near_ref[...] = jnp.dot(rounded, first_pick, preferred_element_type=F32)
    far_ref[...] = jnp.dot(rounded, second_pick, preferred_element_type=F32)

    fold = 8 // channels
    for tile in range(width // LANES):
        lanes = slice(tile * LANES, (tile + 1) * LANES)
        pred = [jnp.zeros((8, LANES), F32) for _ in range(2 * TIME_SLOTS)]
        for row in range(0, per, 8):
            re, im = slice(row, row + 8), slice(per + row, per + row + 8)
            pr, pi, qr, qi = near_ref[re, lanes], near_ref[im, lanes], far_ref[re, lanes], far_ref[im, lanes]
            gr = pr * qr + pi * qi
            gi = pi * qr - pr * qi
            for t in range(TIME_SLOTS):
                mr, mi = model_ref[0, t, re, lanes], model_ref[1, t, re, lanes]
                pred[2 * t] = pred[2 * t] + (gr * mr - gi * mi)
                pred[2 * t + 1] = pred[2 * t + 1] + (gr * mi + gi * mr)
        validity = valid_ref[:, lanes].astype(F32)
        resid = []
        for t in range(TIME_SLOTS):
            for x in range(2):
                p = pred[2 * t + x]
                total = p[0:channels]
                for k in range(1, fold):
                    total = total + p[k * channels:(k + 1) * channels]
                r = (visible_ref[x, t, :, lanes] - total) * validity
                resid.append(jnp.concatenate([r] * fold, axis=0))
        for row in range(0, per, 8):
            re, im = slice(row, row + 8), slice(per + row, per + row + 8)
            third = slice(2 * per + row, 2 * per + row + 8)
            pr, pi, qr, qi = near_ref[re, lanes], near_ref[im, lanes], far_ref[re, lanes], far_ref[im, lanes]
            ar = ai = None
            for t in range(TIME_SLOTS):
                mr, mi = model_ref[0, t, re, lanes], model_ref[1, t, re, lanes]
                rr, ri = resid[2 * t], resid[2 * t + 1]
                br = mr * rr + mi * ri
                bi = mr * ri - mi * rr
                ar, ai = (br, bi) if ar is None else (ar + br, ai + bi)
            power = power_ref[re, lanes]
            upper_ref[re, lanes] = qr * ar - qi * ai
            upper_ref[im, lanes] = qr * ai + qi * ar
            upper_ref[third, lanes] = power * (qr * qr + qi * qi)
            lower_ref[re, lanes] = pr * ar + pi * ai
            lower_ref[im, lanes] = pi * ar - pr * ai
            lower_ref[third, lanes] = power * (pr * pr + pi * pi)
    over = (((1,), (1,)), ((), ()))
    sums_ref[...] += lax.dot_general(
        upper_ref[...].astype(BF16), first_pick, over, preferred_element_type=F32
    ) + lax.dot_general(
        lower_ref[...].astype(BF16), second_pick, over, preferred_element_type=F32
    )

    @pl.when(step == pl.num_programs(0) - 1)
    def _():
        weight = sums_ref[2 * per:3 * per, :] + 1.0 / blocks
        product = partial(jnp.dot, precision=HIGHEST, preferred_element_type=F32)
        normal = product(normal_ref[...], weight)
        right = [
            product(right_ref[...], weight * current_ref[x * per:(x + 1) * per, :] + sums_ref[x * per:(x + 1) * per, :])
            for x in range(2)
        ]
        for half, out in enumerate((own_ref, other_ref)):
            out[0:6 * HALF, :] = normal[half * 6 * HALF:(half + 1) * 6 * HALF, :]
            for x in range(2):
                out[(6 + 3 * x) * HALF:(9 + 3 * x) * HALF, :] = right[x][half * 3 * HALF:(half + 1) * 3 * HALF, :]


def sweep(first, gains, stations, model, power, valid, visible, normal, right, owned, blocks):
    channels, baselines = valid.shape
    per = DIRECTIONS * channels
    chunk = min(SWEEP_CHUNK, baselines)
    count = owned * blocks
    whole = lambda shape: pl.BlockSpec(shape, lambda i: (0,) * len(shape))
    return pl.pallas_call(
        partial(sweep_kernel, first, blocks, owned),
        grid=(baselines // chunk,),
        in_specs=[whole(g.shape) for g in gains] + [
            pl.BlockSpec((2, chunk), lambda i: (0, i)),
            pl.BlockSpec((2, TIME_SLOTS, per, chunk), lambda i: (0, 0, 0, i)),
            pl.BlockSpec((per, chunk), lambda i: (0, i)),
            pl.BlockSpec((channels, chunk), lambda i: (0, i)),
            pl.BlockSpec((2, TIME_SLOTS, channels, chunk), lambda i: (0, 0, 0, i)),
            whole(normal.shape),
            whole(right.shape),
        ],
        out_specs=[whole((12 * HALF, count)), whole((12 * HALF, count)), whole((2 * per, count))],
        out_shape=[
            jax.ShapeDtypeStruct((12 * HALF, count), F32),
            jax.ShapeDtypeStruct((12 * HALF, count), F32),
            jax.ShapeDtypeStruct((2 * per, count), F32),
        ],
        scratch_shapes=[
            pltpu.VMEM((2 * per, count), BF16),
            pltpu.VMEM((3 * per, count), F32),
            pltpu.VMEM((2 * per, chunk), F32),
            pltpu.VMEM((2 * per, chunk), F32),
            pltpu.VMEM((3 * per, chunk), F32),
            pltpu.VMEM((3 * per, chunk), F32),
        ],
        compiler_params=pltpu.CompilerParams(vmem_limit_bytes=40 << 20),
        name="sweep",
    )(*gains, stations, model, power, valid, visible, normal, right)


def final_kernel(channels, before_ref, fit_ref, own_ref, other_ref, out_ref):
    per = DIRECTIONS * channels
    result = 0.5 * (before_ref[...] + fitted_values(fit_ref, (own_ref[...], other_ref[...])))
    for x in range(2):
        for d in range(DIRECTIONS):
            row = x * per + d * channels
            out_ref[x, d] = result[row:row + channels, :]


def finish(before, fit, own, other, channels):
    owned = own.shape[1]
    return pl.pallas_call(
        partial(final_kernel, channels),
        grid=(1,),
        in_specs=[
            pl.BlockSpec((before.shape[0], owned), lambda i: (0, 0)),
            pl.BlockSpec(fit.shape, lambda i: (0, 0, 0)),
            pl.BlockSpec(own.shape, lambda i: (0, 0)),
            pl.BlockSpec(other.shape, lambda i: (0, 0)),
        ],
        out_specs=pl.BlockSpec((2, DIRECTIONS, channels, owned), lambda i: (0, 0, 0, 0)),
        out_shape=jax.ShapeDtypeStruct((2, DIRECTIONS, channels, owned), F32),
        name="finish",
    )(before, fit, own, other)


def solve(moments):
    m = [moments[k * HALF:(k + 1) * HALF] for k in range(12)]
    low_aa = jnp.sqrt(m[0])
    low_ba = m[1] / low_aa
    low_ca = m[2] / low_aa
    low_bb = jnp.sqrt(m[3] - low_ba * low_ba)
    low_cb = (m[4] - low_ca * low_ba) / low_bb
    low_cc = jnp.sqrt(m[5] - low_ca * low_ca - low_cb * low_cb)
    out = []
    for x in range(2):
        r = m[6 + 3 * x:9 + 3 * x]
        first_y = r[0] / low_aa
        second_y = (r[1] - low_ba * first_y) / low_bb
        third_y = (r[2] - low_ca * first_y - low_cb * second_y) / low_cc
        third_x = third_y / low_cc
        second_x = (second_y - low_cb * third_x) / low_bb
        first_x = (first_y - low_ba * second_x - low_ca * third_x) / low_aa
        out += [first_x, second_x, third_x]
    return jnp.concatenate(out, axis=0)


def other_core(value):
    count = lax.axis_size("chan")
    return lax.ppermute(value, "chan", [(j, j ^ 1) for j in range(count)])


def from_later(value, k):
    count = lax.axis_size("bl")
    return lax.ppermute(value, "bl", [((j + k) % count, j) for j in range(count)])


def over_chips(value):
    count = lax.axis_size("chan")
    chips = count // 2
    swap = lambda v, k: lax.ppermute(v, "chan", [(j, j ^ (2 * k)) for j in range(count)])
    if chips <= 4:
        parts = [swap(value, k) for k in range(1, chips)]
        for part in parts:
            value = value + part
        return value
    k = 1
    while k < chips:
        value = value + swap(value, k)
        k *= 2
    return value


def body(patches, visibilities, valid, baseline_stations, cluster, gains):
    channels = visibilities.shape[2]
    owned = gains.shape[3]
    blocks = lax.axis_size("bl")
    total = channels * lax.axis_size("chan")
    all_gains = [gains] + [from_later(gains, k) for k in range(1, blocks)]
    model, power, normal, right, fit = prepare(cluster[:, 0], patches, valid, total)
    common = (baseline_stations, model, power, valid, visibilities, normal, right, owned, blocks)
    inputs = all_gains
    for number in range(ITERS):
        own, other, current = sweep(number == 0, inputs, *common)
        mine = own + other_core(other)
        part = lambda k: mine[:, k * owned:(k + 1) * owned]
        kept = part(0)
        for k in range(1, blocks):
            kept = kept + from_later(part(blocks - k), k)
        coefs = solve(over_chips(kept))
        if number < ITERS - 1:
            coefs = jnp.concatenate([coefs] + [from_later(coefs, k) for k in range(1, blocks)], axis=1)
        inputs = [current, fit, coefs, other_core(coefs)]
    return finish(*inputs, channels)


def solution(mesh):
    in_specs = (
        P(None, None, None, ("grp", "chan"), "bl"),
        P(None, None, ("grp", "chan"), "bl"),
        P(("grp", "chan"), "bl"),
        P(None, "bl"),
        P(),
        P(None, None, ("grp", "chan"), "bl"),
    )
    out_specs = P(None, None, ("grp", "chan"), "bl")
    return jax.shard_map(body, mesh=mesh, in_specs=in_specs, out_specs=out_specs, check_vma=False)
```

```python
from functools import partial

import jax
import jax.numpy as jnp
from jax import lax
from jax.experimental import pallas as pl
from jax.experimental.pallas import tpu as pltpu
from jax.sharding import PartitionSpec as P

DIRECTIONS = 16
SKY_PATCHES = 32
TIME_SLOTS = 2
ITERS = 2
LANES = 128
PREP_CHUNK = 1024
SWEEP_TILE = 256
HALF = DIRECTIONS // 2
HIGHEST = lax.Precision.HIGHEST
F32, BF16 = jnp.float32, jnp.bfloat16


def basis_at(channel, total):
    ratio = 1.0 + channel.astype(F32) / total
    inverse = 4.0 / ratio - 3.0
    return jnp.ones_like(inverse), inverse, 2.0 * inverse * inverse - 1.0


def iotas(shape):
    return lax.broadcasted_iota(jnp.int32, shape, 0), lax.broadcasted_iota(jnp.int32, shape, 1)


def pick(index, values):
    out = values[-1]
    for k in range(len(values) - 2, -1, -1):
        out = jnp.where(index == k, values[k], out)
    return out


def moment_matrix(terms, channels, total, chan):
    row, col = iotas((2 * terms * HALF, DIRECTIONS * channels))
    block = row // HALF
    half = (block >= terms).astype(jnp.int32)
    term = block - half * terms
    direction = jnp.bitwise_xor(half, lax.rem(chan, 2)) * HALF + row % HALF
    one, first, second = basis_at(chan * channels + col % channels, total)
    if terms == 5:
        values = (one, first, second, first * second, second * second)
    else:
        values = (one, first, second)
    return jnp.where(direction == col // channels, pick(term, values), 0.0)


def fit_matrix(half, channels, total, chan):
    per = DIRECTIONS * channels
    row, col = iotas((2 * per, 6 * HALF))
    place = row % per
    block = col // HALF
    direction = jnp.bitwise_xor(half, lax.rem(chan, 2)) * HALF + col % HALF
    basis = basis_at(chan * channels + place % channels, total)
    same = (direction == place // channels) & (row // per == block // 3)
    return jnp.where(same, pick(block % 3, basis), 0.0)


def prep_kernel(total, channels, chunk, cluster_hbm, patches_hbm, valid_hbm, model_ref, power_ref,
                normal_ref, right_ref, fit_ref, patches_ref, valid_ref, cluster_ref, sems, order_ref, start_ref):
    chan = lax.axis_index("chan")
    baselines = valid_ref.shape[1]
    cluster_copy = pltpu.make_async_copy(cluster_hbm, cluster_ref, sems.at[baselines // chunk])
    cluster_copy.start()
    valid_copy = pltpu.make_async_copy(valid_hbm, valid_ref, sems.at[baselines // chunk + 1])
    valid_copy.start()
    copies = []
    for part in range(baselines // chunk):
        here = pl.ds(part * chunk, chunk)
        copies.append(pltpu.make_async_copy(patches_hbm.at[..., here], patches_ref.at[..., here], sems.at[part]))
        copies[-1].start()
    normal_ref[...] = moment_matrix(5, channels, total, chan)
    right_ref[...] = moment_matrix(3, channels, total, chan)
    fit_ref[0] = fit_matrix(0, channels, total, chan)
    fit_ref[1] = fit_matrix(1, channels, total, chan)
    for d in range(DIRECTIONS + 1):
        start_ref[d] = 0
    cluster_copy.wait()

    @pl.loop(0, SKY_PATCHES)
    def _(q):
        d = cluster_ref[q]
        start_ref[d + 1] = start_ref[d + 1] + 1

    for d in range(DIRECTIONS):
        start_ref[d + 1] = start_ref[d + 1] + start_ref[d]
    for d in range(DIRECTIONS):
        start_ref[DIRECTIONS + 1 + d] = start_ref[d]

    @pl.loop(0, SKY_PATCHES)
    def _(q):
        d = cluster_ref[q]
        place = start_ref[DIRECTIONS + 1 + d]
        order_ref[place] = q
        start_ref[DIRECTIONS + 1 + d] = place + 1

    valid_copy.wait()
    fold = 8 // channels
    parts = [(x, t) for x in range(2) for t in range(TIME_SLOTS)]
    for part in range(baselines // chunk):
        copies[part].wait()
        here = slice(part * chunk, (part + 1) * chunk)
        validity = valid_ref[:, here].astype(F32)

        @pl.loop(0, DIRECTIONS // fold)
        def _(group):
            found = []
            for k in range(fold):
                d = group * fold + k

                def add(i, sums):
                    q = order_ref[i]
                    return tuple(
                        s + patches_ref[q, x, t, :, here].astype(F32) for s, (x, t) in zip(sums, parts)
                    )

                zero = jnp.zeros((channels, chunk), F32)
                found.append(lax.fori_loop(start_ref[d], start_ref[d + 1], add, (zero,) * len(parts)))
            rows = pl.ds(pl.multiple_of(group * 8, 8), 8)
            power = None
            for j, (x, t) in enumerate(parts):
                s = jnp.concatenate([f[j] for f in found], axis=0)
                model_ref[x, t, rows, here] = s
                power = s * s if power is None else power + s * s
            power_ref[rows, here] = power * jnp.concatenate([validity] * fold, axis=0)


def prepare(cluster, patches, valid, total):
    channels, baselines = valid.shape
    chunk = min(PREP_CHUNK, baselines)
    per = DIRECTIONS * channels
    vmem = pl.BlockSpec(memory_space=pltpu.VMEM)
    return pl.pallas_call(
        partial(prep_kernel, total, channels, chunk),
        in_specs=[
            pl.BlockSpec(memory_space=pltpu.HBM),
            pl.BlockSpec(memory_space=pltpu.HBM),
            pl.BlockSpec(memory_space=pltpu.HBM),
        ],
        out_specs=[vmem] * 5,
        out_shape=[
            jax.ShapeDtypeStruct((2, TIME_SLOTS, per, baselines), F32),
            jax.ShapeDtypeStruct((per, baselines), F32),
            jax.ShapeDtypeStruct((10 * HALF, per), F32),
            jax.ShapeDtypeStruct((6 * HALF, per), F32),
            jax.ShapeDtypeStruct((2, 2 * per, 6 * HALF), F32),
        ],
        scratch_shapes=[
            pltpu.VMEM(patches.shape, BF16),
            pltpu.VMEM(valid.shape, valid.dtype),
            pltpu.SMEM((SKY_PATCHES,), jnp.int32),
            pltpu.SemaphoreType.DMA((baselines // chunk + 2,)),
            pltpu.SMEM((SKY_PATCHES,), jnp.int32),
            pltpu.SMEM((2 * DIRECTIONS + 1,), jnp.int32),
        ],
        compiler_params=pltpu.CompilerParams(vmem_limit_bytes=32 << 20),
        name="prepare",
    )(*(pltpu.with_memory_space_constraint(v, pltpu.HBM) for v in (cluster, patches, valid)))


def fitted_values(fit_ref, coefs):
    out = jnp.dot(fit_ref[0], coefs[0], precision=HIGHEST, preferred_element_type=F32)
    return out + jnp.dot(fit_ref[1], coefs[1], precision=HIGHEST, preferred_element_type=F32)


def sweep_kernel(first, blocks, owned, tile, *refs):
    if first:
        gain_refs, refs = refs[:blocks], refs[blocks:]
        (stations_ref, model_ref, power_ref, valid_ref, visible_ref, normal_ref, right_ref,
         own_ref, other_ref, current_ref, picks_ref, *refs) = refs
    else:
        (before_ref, fit_ref, own_coef_ref, other_coef_ref, picks_ref), refs = refs[:5], refs[5:]
        (model_ref, power_ref, valid_ref, visible_ref, normal_ref, right_ref,
         own_ref, other_ref, current_ref, *refs) = refs
    rounded_ref, sums_ref, chosen_even, chosen_odd, terms_even, terms_odd = refs
    chosen_refs, terms_refs = (chosen_even, chosen_odd), (terms_even, terms_odd)
    channels, baselines = valid_ref.shape
    per = DIRECTIONS * channels
    stations = blocks * owned
    fold = 8 // channels
    if first:
        for k in range(blocks):
            for x in range(2):
                for d in range(0, DIRECTIONS, fold):
                    row = x * per + d * channels
                    pair = jnp.concatenate([gain_refs[k][x, d + j] for j in range(fold)], axis=0)
                    current_ref[row:row + 8, k * owned:(k + 1) * owned] = pair
    else:
        fitted = fitted_values(fit_ref, (own_coef_ref[...], other_coef_ref[...]))
        current_ref[...] = 0.5 * (before_ref[...] + fitted)
    rounded_ref[...] = current_ref[...].astype(BF16)

    def span(i, width):
        if isinstance(i, int):
            return slice(i * width, (i + 1) * width)
        return pl.ds(pl.multiple_of(i * width, width), width)

    def choose(i, slot):
        here = span(i, 2 * tile)
        if first:
            shift = lax.axis_index("bl") * owned
            place = stations_ref[:, span(i, tile)] - shift
            place = jnp.where(place < 0, place + stations, place)
            place = jnp.concatenate([place[0:1, :], place[1:2, :]], axis=1)
            ids = lax.broadcasted_iota(jnp.int32, (stations, 2 * tile), 0)
            picks_ref[:, here] = (ids == place).astype(BF16)
        chosen_refs[slot][...] = jnp.dot(rounded_ref[...], picks_ref[:, here], preferred_element_type=F32)

    def terms(i, slot):
        chosen_ref, terms_ref = chosen_refs[slot], terms_refs[slot]
        for part in range(tile // LANES):
            near, far = (slice(k * tile + part * LANES, k * tile + (part + 1) * LANES) for k in range(2))
            if isinstance(i, int):
                along = slice(i * tile + part * LANES, i * tile + (part + 1) * LANES)
            else:
                along = pl.ds(pl.multiple_of(i * tile + part * LANES, LANES), LANES)
            pred = [jnp.zeros((8, LANES), F32) for _ in range(2 * TIME_SLOTS)]
            for row in range(0, per, 8):
                re, im = slice(row, row + 8), slice(per + row, per + row + 8)
                pr, pi, qr, qi = chosen_ref[re, near], chosen_ref[im, near], chosen_ref[re, far], chosen_ref[im, far]
                gr = pr * qr + pi * qi
                gi = pi * qr - pr * qi
                for t in range(TIME_SLOTS):
                    mr, mi = model_ref[0, t, re, along], model_ref[1, t, re, along]
                    pred[2 * t] = pred[2 * t] + (gr * mr - gi * mi)
                    pred[2 * t + 1] = pred[2 * t + 1] + (gr * mi + gi * mr)
            validity = valid_ref[:, along].astype(F32)
            resid = []
            for t in range(TIME_SLOTS):
                for x in range(2):
                    p = pred[2 * t + x]
                    total = p[0:channels]
                    for k in range(1, fold):
                        total = total + p[k * channels:(k + 1) * channels]
                    r = (visible_ref[x, t, :, along] - total) * validity
                    resid.append(jnp.concatenate([r] * fold, axis=0))
            rows = [[None] * (per // 8) for _ in range(6)]
            for row in range(0, per, 8):
                re, im = slice(row, row + 8), slice(per + row, per + row + 8)
                pr, pi, qr, qi = chosen_ref[re, near], chosen_ref[im, near], chosen_ref[re, far], chosen_ref[im, far]
                ar = ai = None
                for t in range(TIME_SLOTS):
                    mr, mi = model_ref[0, t, re, along], model_ref[1, t, re, along]
                    rr, ri = resid[2 * t], resid[2 * t + 1]
                    br = mr * rr + mi * ri
                    bi = mr * ri - mi * rr
                    ar, ai = (br, bi) if ar is None else (ar + br, ai + bi)
                power = power_ref[re, along]
                values = (qr * ar - qi * ai, qr * ai + qi * ar, power * (qr * qr + qi * qi),
                          pr * ar + pi * ai, pi * ar - pr * ai, power * (pr * pr + pi * pi))
                for k in range(6):
                    rows[k][row // 8] = values[k]
                if row % 16 == 8:
                    for k in range(6):
                        two = jnp.concatenate(rows[k][row // 8 - 1:row // 8 + 1], axis=0).astype(BF16)
                        terms_ref[(k % 3) * per + row - 8:(k % 3) * per + row + 8, (near, far)[k // 3]] = two

    def add_up(i, slot):
        more = lax.dot_general(
            picks_ref[:, span(i, 2 * tile)], terms_refs[slot][...], (((1,), (1,)), ((), ())),
            preferred_element_type=F32,
        )
        if isinstance(i, int) and i == 0:
            sums_ref[...] = more
        else:
            sums_ref[...] += more

    count = baselines // tile
    choose(0, 0)
    choose(1, 1)
    terms(0, 0)
    add_up(0, 0)
    choose(2, 0)
    terms(1, 1)

    @pl.loop(0, (count - 4) // 2)
    def _(j):
        i = 2 * j + 3
        for k in range(2):
            add_up(i + k - 2, 1 - k)
            choose(i + k, 1 - k)
            terms(i + k - 1, k)

    for i in range(count - 1, count):
        add_up(i - 2, i % 2)
        choose(i, i % 2)
        terms(i - 1, 1 - i % 2)
    add_up(count - 2, count % 2)
    terms(count - 1, 1 - count % 2)
    add_up(count - 1, 1 - count % 2)

    sums = sums_ref[...].T
    weight = sums[2 * per:3 * per, :] + 1.0 / blocks
    product = partial(jnp.dot, precision=HIGHEST, preferred_element_type=F32)
    normal = product(normal_ref[...], weight)
    right = [
        product(right_ref[...], weight * current_ref[x * per:(x + 1) * per, :] + sums[x * per:(x + 1) * per, :])
        for x in range(2)
    ]
    for half, out in enumerate((own_ref, other_ref)):
        out[0:5 * HALF, :] = normal[half * 5 * HALF:(half + 1) * 5 * HALF, :]
        for x in range(2):
            out[(5 + 3 * x) * HALF:(8 + 3 * x) * HALF, :] = right[x][half * 3 * HALF:(half + 1) * 3 * HALF, :]


def sweep(first, inputs, model, power, valid, visible, normal, right, owned, blocks):
    channels, baselines = valid.shape
    per = DIRECTIONS * channels
    count = owned * blocks
    vmem = pl.BlockSpec(memory_space=pltpu.VMEM)
    outs = [
        jax.ShapeDtypeStruct((11 * HALF, count), F32),
        jax.ShapeDtypeStruct((11 * HALF, count), F32),
        jax.ShapeDtypeStruct((2 * per, count), F32),
    ]
    if first:
        outs.append(jax.ShapeDtypeStruct((count, 2 * baselines), BF16))
    return pl.pallas_call(
        partial(sweep_kernel, first, blocks, owned, SWEEP_TILE),
        in_specs=[vmem] * (len(inputs) + 6),
        out_specs=[vmem] * len(outs),
        out_shape=outs,
        scratch_shapes=[
            pltpu.VMEM((2 * per, count), BF16),
            pltpu.VMEM((count, 3 * per), F32),
            pltpu.VMEM((2 * per, 2 * SWEEP_TILE), F32),
            pltpu.VMEM((2 * per, 2 * SWEEP_TILE), F32),
            pltpu.VMEM((3 * per, 2 * SWEEP_TILE), BF16),
            pltpu.VMEM((3 * per, 2 * SWEEP_TILE), BF16),
        ],
        compiler_params=pltpu.CompilerParams(vmem_limit_bytes=24 << 20),
        name="sweep",
    )(*inputs, model, power, valid, visible, normal, right)


def final_kernel(channels, before_ref, fit_ref, own_ref, other_ref, out_ref):
    per = DIRECTIONS * channels
    result = 0.5 * (before_ref[:, 0:out_ref.shape[3]] + fitted_values(fit_ref, (own_ref[...], other_ref[...])))
    for x in range(2):
        for d in range(DIRECTIONS):
            row = x * per + d * channels
            out_ref[x, d] = result[row:row + channels, :]


def finish(before, fit, own, other, channels):
    owned = own.shape[1]
    return pl.pallas_call(
        partial(final_kernel, channels),
        in_specs=[pl.BlockSpec(memory_space=pltpu.VMEM)] * 4,
        out_specs=pl.BlockSpec(memory_space=pltpu.VMEM),
        out_shape=jax.ShapeDtypeStruct((2, DIRECTIONS, channels, owned), F32),
        compiler_params=pltpu.CompilerParams(vmem_limit_bytes=8 << 20),
        name="finish",
    )(before, fit, own, other)


def solve(moments):
    m = [moments[k * HALF:(k + 1) * HALF] for k in range(11)]
    m.insert(3, 0.5 * (m[0] + m[2]))
    low_aa = jnp.sqrt(m[0])
    low_ba = m[1] / low_aa
    low_ca = m[2] / low_aa
    low_bb = jnp.sqrt(m[3] - low_ba * low_ba)
    low_cb = (m[4] - low_ca * low_ba) / low_bb
    low_cc = jnp.sqrt(m[5] - low_ca * low_ca - low_cb * low_cb)
    out = []
    for x in range(2):
        r = m[6 + 3 * x:9 + 3 * x]
        first_y = r[0] / low_aa
        second_y = (r[1] - low_ba * first_y) / low_bb
        third_y = (r[2] - low_ca * first_y - low_cb * second_y) / low_cc
        third_x = third_y / low_cc
        second_x = (second_y - low_cb * third_x) / low_bb
        first_x = (first_y - low_ba * second_x - low_ca * third_x) / low_aa
        out += [first_x, second_x, third_x]
    return jnp.concatenate(out, axis=0)


def other_core(value):
    count = lax.axis_size("chan")
    return lax.ppermute(value, "chan", [(j, j ^ 1) for j in range(count)])


def from_later(value, k):
    count = lax.axis_size("bl")
    return lax.ppermute(value, "bl", [((j + k) % count, j) for j in range(count)])


def over_chips(value):
    count = lax.axis_size("chan")
    chips = count // 2
    swap = lambda v, k: lax.ppermute(v, "chan", [(j, j ^ (2 * k)) for j in range(count)])
    if chips <= 4:
        parts = [swap(value, k) for k in range(1, chips)]
        for part in parts:
            value = value + part
        return value
    k = 1
    while k < chips:
        value = value + swap(value, k)
        k *= 2
    return value


def body(patches, visibilities, valid, baseline_stations, cluster, gains):
    channels = visibilities.shape[2]
    owned = gains.shape[3]
    blocks = lax.axis_size("bl")
    total = channels * lax.axis_size("chan")
    all_gains = [gains] + [from_later(gains, k) for k in range(1, blocks)]
    model, power, normal, right, fit = prepare(cluster[:, 0], patches, valid, total)
    common = (model, power, valid, visibilities, normal, right, owned, blocks)
    inputs = all_gains + [baseline_stations]
    picks = None
    for number in range(ITERS):
        own, other, current, *made = sweep(number == 0, inputs, *common)
        picks = made[0] if made else picks
        mine = own + other_core(other)
        part = lambda k: mine[:, k * owned:(k + 1) * owned]
        kept = part(0)
        for k in range(1, blocks):
            kept = kept + from_later(part(blocks - k), k)
        coefs = solve(over_chips(kept))
        if number < ITERS - 1:
            coefs = jnp.concatenate([coefs] + [from_later(coefs, k) for k in range(1, blocks)], axis=1)
        inputs = [current, fit, coefs, other_core(coefs), picks]
    return finish(*inputs[:4], channels)


def solution(mesh):
    in_specs = (
        P(None, None, None, ("grp", "chan"), "bl"),
        P(None, None, ("grp", "chan"), "bl"),
        P(("grp", "chan"), "bl"),
        P(None, "bl"),
        P(),
        P(None, None, ("grp", "chan"), "bl"),
    )
    out_specs = P(None, None, ("grp", "chan"), "bl")
    return jax.shard_map(body, mesh=mesh, in_specs=in_specs, out_specs=out_specs, check_vma=False)
```

```python
from functools import partial

import jax
import jax.numpy as jnp
from jax import lax
from jax.experimental import pallas as pl
from jax.experimental.pallas import tpu as pltpu
from jax.sharding import PartitionSpec as P

DIRECTIONS = 16
SKY_PATCHES = 32
TIME_SLOTS = 2
ITERS = 2
LANES = 128
EXACT = 256
PREP_CHUNK = 1024
SWEEP_TILE = 1024
HALF = DIRECTIONS // 2
HIGHEST = lax.Precision.HIGHEST
F32, BF16 = jnp.float32, jnp.bfloat16


def basis_at(channel, total):
    ratio = 1.0 + channel.astype(F32) / total
    inverse = 4.0 / ratio - 3.0
    return jnp.ones_like(inverse), inverse, 2.0 * inverse * inverse - 1.0


def iotas(shape):
    return lax.broadcasted_iota(jnp.int32, shape, 0), lax.broadcasted_iota(jnp.int32, shape, 1)


def pick(index, values):
    out = values[-1]
    for k in range(len(values) - 2, -1, -1):
        out = jnp.where(index == k, values[k], out)
    return out


def moment_matrix(terms, channels, total, chan):
    row, col = iotas((2 * terms * HALF, DIRECTIONS * channels))
    block = row // HALF
    half = (block >= terms).astype(jnp.int32)
    term = block - half * terms
    direction = jnp.bitwise_xor(half, lax.rem(chan, 2)) * HALF + row % HALF
    one, first, second = basis_at(chan * channels + col % channels, total)
    if terms == 5:
        values = (one, first, second, first * second, second * second)
    else:
        values = (one, first, second)
    return jnp.where(direction == col // channels, pick(term, values), 0.0)


def fit_matrix(channels, total, chan):
    per = DIRECTIONS * channels
    row, col = iotas((2 * per, 12 * HALF))
    place = row % per
    block = col // HALF
    half = (block >= 6).astype(jnp.int32)
    block = block - 6 * half
    direction = jnp.bitwise_xor(half, lax.rem(chan, 2)) * HALF + col % HALF
    basis = basis_at(chan * channels + place % channels, total)
    same = (direction == place // channels) & (row // per == block // 3)
    return jnp.where(same, pick(block % 3, basis), 0.0)


def prep_kernel(total, channels, chunk, cluster_hbm, patches_hbm, valid_hbm, model_ref, power_ref,
                normal_ref, right_ref, fit_ref, patches_ref, valid_ref, cluster_ref, sems, order_ref, start_ref):
    chan = lax.axis_index("chan")
    baselines = valid_ref.shape[1]
    cluster_copy = pltpu.make_async_copy(cluster_hbm, cluster_ref, sems.at[baselines // chunk])
    cluster_copy.start()
    valid_copy = pltpu.make_async_copy(valid_hbm, valid_ref, sems.at[baselines // chunk + 1])
    valid_copy.start()
    copies = []
    rows = channels * chunk // LANES
    for part in range(baselines // chunk):
        here = pl.ds(part * rows, rows)
        copies.append(pltpu.make_async_copy(patches_hbm.at[:, :, :, here], patches_ref.at[:, :, :, here], sems.at[part]))
        copies[-1].start()
    normal_ref[...] = moment_matrix(5, channels, total, chan)
    right_ref[...] = moment_matrix(3, channels, total, chan)
    fit_ref[...] = fit_matrix(channels, total, chan)
    for d in range(DIRECTIONS + 1):
        start_ref[d] = 0
    cluster_copy.wait()

    @pl.loop(0, SKY_PATCHES)
    def _(q):
        d = cluster_ref[q]
        start_ref[d + 1] = start_ref[d + 1] + 1

    for d in range(DIRECTIONS):
        start_ref[d + 1] = start_ref[d + 1] + start_ref[d]
    for d in range(DIRECTIONS):
        start_ref[DIRECTIONS + 1 + d] = start_ref[d]

    @pl.loop(0, SKY_PATCHES)
    def _(q):
        d = cluster_ref[q]
        place = start_ref[DIRECTIONS + 1 + d]
        order_ref[place] = q
        start_ref[DIRECTIONS + 1 + d] = place + 1

    valid_copy.wait()
    fold = 8 // channels
    parts = [(x, t) for x in range(2) for t in range(TIME_SLOTS)]
    for part in range(baselines // chunk):
        copies[part].wait()
        own_rows = slice(part * rows, (part + 1) * rows)

        @pl.loop(0, DIRECTIONS // fold)
        def _(group):
            found = []
            for k in range(fold):
                d = group * fold + k

                def patch(i):
                    q = order_ref[i]
                    return tuple(patches_ref[q, x, t, own_rows, :].astype(F32) for x, t in parts)

                def add(i, sums):
                    return tuple(s + p for s, p in zip(sums, patch(i)))

                found.append(lax.fori_loop(start_ref[d] + 1, start_ref[d + 1], add, patch(start_ref[d])))
            place = pl.ds(pl.multiple_of(group * 8, 8), 8)
            for tile in range(chunk // LANES):
                here = slice(part * chunk + tile * LANES, part * chunk + (tile + 1) * LANES)
                mine = slice(tile * channels, (tile + 1) * channels)
                power = None
                for j, (x, t) in enumerate(parts):
                    s = jnp.concatenate([f[j][mine] for f in found], axis=0)
                    model_ref[x, t, place, here] = s
                    power = s * s if power is None else power + s * s
                validity = valid_ref[:, here].astype(F32)
                power_ref[place, here] = power * jnp.concatenate([validity] * fold, axis=0)


def prepare(cluster, patches, valid, total):
    channels, baselines = valid.shape
    lead = patches.shape[:3]
    tiled = patches.reshape(*lead, channels, baselines // LANES, LANES)
    tiled = jnp.swapaxes(tiled, 3, 4).reshape(*lead, channels * baselines // LANES, LANES)
    chunk = min(PREP_CHUNK, baselines)
    per = DIRECTIONS * channels
    vmem = pl.BlockSpec(memory_space=pltpu.VMEM)
    return pl.pallas_call(
        partial(prep_kernel, total, channels, chunk),
        in_specs=[
            pl.BlockSpec(memory_space=pltpu.HBM),
            pl.BlockSpec(memory_space=pltpu.HBM),
            pl.BlockSpec(memory_space=pltpu.HBM),
        ],
        out_specs=[vmem] * 5,
        out_shape=[
            jax.ShapeDtypeStruct((2, TIME_SLOTS, per, baselines), F32),
            jax.ShapeDtypeStruct((per, baselines), F32),
            jax.ShapeDtypeStruct((10 * HALF, per), F32),
            jax.ShapeDtypeStruct((6 * HALF, per), F32),
            jax.ShapeDtypeStruct((2 * per, 12 * HALF), F32),
        ],
        scratch_shapes=[
            pltpu.VMEM(tiled.shape, BF16),
            pltpu.VMEM(valid.shape, valid.dtype),
            pltpu.SMEM((SKY_PATCHES,), jnp.int32),
            pltpu.SemaphoreType.DMA((baselines // chunk + 2,)),
            pltpu.SMEM((SKY_PATCHES,), jnp.int32),
            pltpu.SMEM((2 * DIRECTIONS + 1,), jnp.int32),
        ],
        compiler_params=pltpu.CompilerParams(vmem_limit_bytes=32 << 20),
        name="prepare",
    )(*(pltpu.with_memory_space_constraint(v, pltpu.HBM) for v in (cluster, tiled, valid)))


def fitted_values(fit_ref, own_ref, other_ref):
    coefs = jnp.concatenate([own_ref[...], other_ref[...]], axis=0)
    return jnp.dot(fit_ref[...], coefs, precision=HIGHEST, preferred_element_type=F32)


def sweep_kernel(first, blocks, owned, tile, *refs):
    if first:
        gain_refs, refs = refs[:blocks], refs[blocks:]
        (stations_ref, model_ref, power_ref, valid_ref, visible_ref, normal_ref, right_ref,
         own_ref, other_ref, current_ref, picks_ref, *refs) = refs
    else:
        (before_ref, fit_ref, own_coef_ref, other_coef_ref, picks_ref), refs = refs[:5], refs[5:]
        (model_ref, power_ref, valid_ref, visible_ref, normal_ref, right_ref,
         own_ref, other_ref, current_ref, *refs) = refs
    rounded_ref, sums_ref, chosen_ref, terms_ref, ids_ref = refs
    if first:
        ids_ref[...] = iotas(ids_ref.shape)[0].astype(F32).astype(BF16)
    channels, baselines = valid_ref.shape
    per = DIRECTIONS * channels
    stations = blocks * owned
    fold = 8 // channels
    if first:
        for k in range(blocks):
            for x in range(2):
                for d in range(0, DIRECTIONS, fold):
                    row = x * per + d * channels
                    pair = jnp.concatenate([gain_refs[k][x, d + j] for j in range(fold)], axis=0)
                    current_ref[row:row + 8, k * owned:(k + 1) * owned] = pair
    else:
        fitted = fitted_values(fit_ref, own_coef_ref, other_coef_ref)
        current_ref[...] = 0.5 * (before_ref[...] + fitted)
    rounded_ref[...] = current_ref[...].astype(BF16)

    def span(i, width):
        if isinstance(i, int):
            return slice(i * width, (i + 1) * width)
        return pl.ds(pl.multiple_of(i * width, width), width)

    def choose(i):
        here = span(i, 2 * tile)
        if first:
            shift = lax.axis_index("bl") * owned
            place = stations_ref[:, span(i, tile)] - shift
            place = jnp.where(place < 0, place + stations, place)
            columns = []
            for part in range(tile // LANES):
                columns += [place[k:k + 1, part * LANES:(part + 1) * LANES] for k in range(2)]
            place = jnp.concatenate(columns, axis=1)
            ids = ids_ref[...]
            for start in range(0, stations, EXACT):
                local = jnp.where((place >= start) & (place < start + EXACT), place - start, -1)
                local = local.astype(F32).astype(BF16)
                picks_ref[start:start + EXACT, here] = jnp.where(ids == local, jnp.ones((), BF16), jnp.zeros((), BF16))
        chosen_ref[...] = jnp.dot(rounded_ref[...], picks_ref[:, here], preferred_element_type=F32)

    def terms(i):
        for part in range(tile // LANES):
            near, far = (slice((2 * part + k) * LANES, (2 * part + k + 1) * LANES) for k in range(2))
            if isinstance(i, int):
                along = slice(i * tile + part * LANES, i * tile + (part + 1) * LANES)
            else:
                along = pl.ds(pl.multiple_of(i * tile + part * LANES, LANES), LANES)
            pred = [jnp.zeros((8, LANES), F32) for _ in range(2 * TIME_SLOTS)]
            for row in range(0, per, 8):
                re, im = slice(row, row + 8), slice(per + row, per + row + 8)
                pr, pi, qr, qi = chosen_ref[re, near], chosen_ref[im, near], chosen_ref[re, far], chosen_ref[im, far]
                gr = pr * qr + pi * qi
                gi = pi * qr - pr * qi
                for t in range(TIME_SLOTS):
                    mr, mi = model_ref[0, t, re, along], model_ref[1, t, re, along]
                    pred[2 * t] = pred[2 * t] + (gr * mr - gi * mi)
                    pred[2 * t + 1] = pred[2 * t + 1] + (gr * mi + gi * mr)
            validity = valid_ref[:, along].astype(F32)
            resid = []
            for t in range(TIME_SLOTS):
                for x in range(2):
                    p = pred[2 * t + x]
                    total = p[0:channels]
                    for k in range(1, fold):
                        total = total + p[k * channels:(k + 1) * channels]
                    r = (visible_ref[x, t, :, along] - total) * validity
                    resid.append(jnp.concatenate([r] * fold, axis=0))
            rows = [[None] * (per // 8) for _ in range(6)]
            for row in range(0, per, 8):
                re, im = slice(row, row + 8), slice(per + row, per + row + 8)
                pr, pi, qr, qi = chosen_ref[re, near], chosen_ref[im, near], chosen_ref[re, far], chosen_ref[im, far]
                ar = ai = None
                for t in range(TIME_SLOTS):
                    mr, mi = model_ref[0, t, re, along], model_ref[1, t, re, along]
                    rr, ri = resid[2 * t], resid[2 * t + 1]
                    br = mr * rr + mi * ri
                    bi = mr * ri - mi * rr
                    ar, ai = (br, bi) if ar is None else (ar + br, ai + bi)
                power = power_ref[re, along]
                values = (qr * ar - qi * ai, qr * ai + qi * ar, power * (qr * qr + qi * qi),
                          pr * ar + pi * ai, pi * ar - pr * ai, power * (pr * pr + pi * pi))
                for k in range(6):
                    rows[k][row // 8] = values[k]
                if row % 16 == 8:
                    for k in range(6):
                        two = jnp.concatenate(rows[k][row // 8 - 1:row // 8 + 1], axis=0).astype(BF16)
                        terms_ref[(k % 3) * per + row - 8:(k % 3) * per + row + 8, (near, far)[k // 3]] = two

    def add_up(i):
        more = lax.dot_general(
            picks_ref[:, span(i, 2 * tile)], terms_ref[...], (((1,), (1,)), ((), ())),
            preferred_element_type=F32,
        )
        if isinstance(i, int) and i == 0:
            sums_ref[...] = more
        else:
            sums_ref[...] += more

    count = baselines // tile
    choose(0)
    terms(0)
    choose(1)
    add_up(0)
    terms(1)
    choose(2)

    @pl.loop(3, count)
    def _(i):
        add_up(i - 2)
        terms(i - 1)
        choose(i)

    add_up(count - 2)
    terms(count - 1)
    add_up(count - 1)

    sums = sums_ref[...].T
    weight = sums[2 * per:3 * per, :] + 1.0 / blocks
    product = partial(jnp.dot, precision=HIGHEST, preferred_element_type=F32)
    normal = product(normal_ref[...], weight)
    right = [
        product(right_ref[...], weight * current_ref[x * per:(x + 1) * per, :] + sums[x * per:(x + 1) * per, :])
        for x in range(2)
    ]
    for half, out in enumerate((own_ref, other_ref)):
        out[0:5 * HALF, :] = normal[half * 5 * HALF:(half + 1) * 5 * HALF, :]
        for x in range(2):
            out[(5 + 3 * x) * HALF:(8 + 3 * x) * HALF, :] = right[x][half * 3 * HALF:(half + 1) * 3 * HALF, :]


def sweep(first, inputs, model, power, valid, visible, normal, right, owned, blocks):
    channels, baselines = valid.shape
    per = DIRECTIONS * channels
    count = owned * blocks
    vmem = pl.BlockSpec(memory_space=pltpu.VMEM)
    outs = [
        jax.ShapeDtypeStruct((11 * HALF, count), F32),
        jax.ShapeDtypeStruct((11 * HALF, count), F32),
        jax.ShapeDtypeStruct((2 * per, count), F32),
    ]
    if first:
        outs.append(jax.ShapeDtypeStruct((count, 2 * baselines), BF16))
    return pl.pallas_call(
        partial(sweep_kernel, first, blocks, owned, SWEEP_TILE),
        in_specs=[vmem] * (len(inputs) + 6),
        out_specs=[vmem] * len(outs),
        out_shape=outs,
        scratch_shapes=[
            pltpu.VMEM((2 * per, count), BF16),
            pltpu.VMEM((count, 3 * per), F32),
            pltpu.VMEM((2 * per, 2 * SWEEP_TILE), F32),
            pltpu.VMEM((3 * per, 2 * SWEEP_TILE), BF16),
            pltpu.VMEM((EXACT, 2 * SWEEP_TILE), BF16),
        ],
        compiler_params=pltpu.CompilerParams(vmem_limit_bytes=24 << 20),
        name="sweep",
    )(*inputs, model, power, valid, visible, normal, right)


def final_kernel(channels, before_ref, fit_ref, own_ref, other_ref, out_ref):
    per = DIRECTIONS * channels
    result = 0.5 * (before_ref[:, 0:out_ref.shape[3]] + fitted_values(fit_ref, own_ref, other_ref))
    for x in range(2):
        for d in range(DIRECTIONS):
            row = x * per + d * channels
            out_ref[x, d] = result[row:row + channels, :]


def finish(before, fit, own, other, channels):
    owned = own.shape[1]
    return pl.pallas_call(
        partial(final_kernel, channels),
        in_specs=[pl.BlockSpec(memory_space=pltpu.VMEM)] * 4,
        out_specs=pl.BlockSpec(memory_space=pltpu.VMEM),
        out_shape=jax.ShapeDtypeStruct((2, DIRECTIONS, channels, owned), F32),
        compiler_params=pltpu.CompilerParams(vmem_limit_bytes=8 << 20),
        name="finish",
    )(before, fit, own, other)


def solve(moments):
    m = [moments[k * HALF:(k + 1) * HALF] for k in range(11)]
    m.insert(3, 0.5 * (m[0] + m[2]))
    low_aa = jnp.sqrt(m[0])
    low_ba = m[1] / low_aa
    low_ca = m[2] / low_aa
    low_bb = jnp.sqrt(m[3] - low_ba * low_ba)
    low_cb = (m[4] - low_ca * low_ba) / low_bb
    low_cc = jnp.sqrt(m[5] - low_ca * low_ca - low_cb * low_cb)
    out = []
    for x in range(2):
        r = m[6 + 3 * x:9 + 3 * x]
        first_y = r[0] / low_aa
        second_y = (r[1] - low_ba * first_y) / low_bb
        third_y = (r[2] - low_ca * first_y - low_cb * second_y) / low_cc
        third_x = third_y / low_cc
        second_x = (second_y - low_cb * third_x) / low_bb
        first_x = (first_y - low_ba * second_x - low_ca * third_x) / low_aa
        out += [first_x, second_x, third_x]
    return jnp.concatenate(out, axis=0)


def other_core(value):
    count = lax.axis_size("chan")
    return lax.ppermute(value, "chan", [(j, j ^ 1) for j in range(count)])


def from_later(value, k):
    count = lax.axis_size("bl")
    return lax.ppermute(value, "bl", [((j + k) % count, j) for j in range(count)])


def over_chips(value):
    count = lax.axis_size("chan")
    chips = count // 2
    swap = lambda v, k: lax.ppermute(v, "chan", [(j, j ^ (2 * k)) for j in range(count)])
    if chips <= 4:
        parts = [swap(value, k) for k in range(1, chips)]
        for part in parts:
            value = value + part
        return value
    k = 1
    while k < chips:
        value = value + swap(value, k)
        k *= 2
    return value


def body(patches, visibilities, valid, baseline_stations, cluster, gains):
    channels = visibilities.shape[2]
    owned = gains.shape[3]
    blocks = lax.axis_size("bl")
    total = channels * lax.axis_size("chan")
    all_gains = [gains] + [from_later(gains, k) for k in range(1, blocks)]
    model, power, normal, right, fit = prepare(cluster[:, 0], patches, valid, total)
    common = (model, power, valid, visibilities, normal, right, owned, blocks)
    inputs = all_gains + [baseline_stations]
    picks = None
    for number in range(ITERS):
        own, other, current, *made = sweep(number == 0, inputs, *common)
        picks = made[0] if made else picks
        mine = own + other_core(other)
        part = lambda k: mine[:, k * owned:(k + 1) * owned]
        kept = part(0)
        for k in range(1, blocks):
            kept = kept + from_later(part(blocks - k), k)
        coefs = solve(over_chips(kept))
        if number < ITERS - 1:
            coefs = jnp.concatenate([coefs] + [from_later(coefs, k) for k in range(1, blocks)], axis=1)
        inputs = [current, fit, coefs, other_core(coefs), picks]
    return finish(*inputs[:4], channels)


def solution(mesh):
    in_specs = (
        P(None, None, None, ("grp", "chan"), "bl"),
        P(None, None, ("grp", "chan"), "bl"),
        P(("grp", "chan"), "bl"),
        P(None, "bl"),
        P(),
        P(None, None, ("grp", "chan"), "bl"),
    )
    out_specs = P(None, None, ("grp", "chan"), "bl")
    return jax.shard_map(body, mesh=mesh, in_specs=in_specs, out_specs=out_specs, check_vma=False)
```

```python
from functools import partial

import jax
import jax.numpy as jnp
from jax import lax
from jax.experimental import pallas as pl
from jax.experimental.pallas import tpu as pltpu
from jax.sharding import PartitionSpec as P

DIRECTIONS = 16
SKY_PATCHES = 32
TIME_SLOTS = 2
ITERS = 2
LANES = 128
EXACT = 256
PREP_CHUNK = 1024
SWEEP_TILE = 1024
OWN_CHUNK = 2048
HALF = DIRECTIONS // 2
HIGHEST = lax.Precision.HIGHEST
F32, BF16 = jnp.float32, jnp.bfloat16


def basis_at(channel, total):
    ratio = 1.0 + channel.astype(F32) / total
    inverse = 4.0 / ratio - 3.0
    return jnp.ones_like(inverse), inverse, 2.0 * inverse * inverse - 1.0


def iotas(shape):
    return lax.broadcasted_iota(jnp.int32, shape, 0), lax.broadcasted_iota(jnp.int32, shape, 1)


def pick(index, values):
    out = values[-1]
    for k in range(len(values) - 2, -1, -1):
        out = jnp.where(index == k, values[k], out)
    return out


def moment_matrix(terms, channels, total, chan):
    row, col = iotas((2 * terms * HALF, DIRECTIONS * channels))
    block = row // HALF
    half = (block >= terms).astype(jnp.int32)
    term = block - half * terms
    direction = jnp.bitwise_xor(half, lax.rem(chan, 2)) * HALF + row % HALF
    one, first, second = basis_at(chan * channels + col % channels, total)
    if terms == 5:
        values = (one, first, second, first * second, second * second)
    else:
        values = (one, first, second)
    return jnp.where(direction == col // channels, pick(term, values), 0.0)


def fit_matrix(channels, total, chan):
    per = DIRECTIONS * channels
    row, col = iotas((2 * per, 12 * HALF))
    place = row % per
    block = col // HALF
    half = (block >= 6).astype(jnp.int32)
    block = block - 6 * half
    direction = jnp.bitwise_xor(half, lax.rem(chan, 2)) * HALF + col % HALF
    basis = basis_at(chan * channels + place % channels, total)
    same = (direction == place // channels) & (row // per == block // 3)
    return jnp.where(same, pick(block % 3, basis), 0.0)


def prep_kernel(total, channels, chunk, cluster_hbm, patches_hbm, valid_hbm, model_ref, power_ref,
                normal_ref, right_ref, fit_ref, patches_ref, valid_ref, cluster_ref, sems, order_ref, start_ref):
    chan = lax.axis_index("chan")
    baselines = valid_ref.shape[1]
    cluster_copy = pltpu.make_async_copy(cluster_hbm, cluster_ref, sems.at[baselines // chunk])
    cluster_copy.start()
    valid_copy = pltpu.make_async_copy(valid_hbm, valid_ref, sems.at[baselines // chunk + 1])
    valid_copy.start()
    copies = []
    rows = channels * chunk // LANES
    for part in range(baselines // chunk):
        here = pl.ds(part * rows, rows)
        copies.append(pltpu.make_async_copy(patches_hbm.at[:, :, :, here], patches_ref.at[:, :, :, here], sems.at[part]))
        copies[-1].start()
    normal_ref[...] = moment_matrix(5, channels, total, chan)
    right_ref[...] = moment_matrix(3, channels, total, chan)
    fit_ref[...] = fit_matrix(channels, total, chan)
    for d in range(DIRECTIONS + 1):
        start_ref[d] = 0
    cluster_copy.wait()

    @pl.loop(0, SKY_PATCHES)
    def _(q):
        d = cluster_ref[q]
        start_ref[d + 1] = start_ref[d + 1] + 1

    for d in range(DIRECTIONS):
        start_ref[d + 1] = start_ref[d + 1] + start_ref[d]
    for d in range(DIRECTIONS):
        start_ref[DIRECTIONS + 1 + d] = start_ref[d]

    @pl.loop(0, SKY_PATCHES)
    def _(q):
        d = cluster_ref[q]
        place = start_ref[DIRECTIONS + 1 + d]
        order_ref[place] = q
        start_ref[DIRECTIONS + 1 + d] = place + 1

    valid_copy.wait()
    fold = 8 // channels
    parts = [(x, t) for x in range(2) for t in range(TIME_SLOTS)]
    for part in range(baselines // chunk):
        copies[part].wait()
        own_rows = slice(part * rows, (part + 1) * rows)

        @pl.loop(0, DIRECTIONS // fold)
        def _(group):
            found = []
            for k in range(fold):
                d = group * fold + k

                def patch(i):
                    q = order_ref[i]
                    return tuple(patches_ref[q, x, t, own_rows, :].astype(F32) for x, t in parts)

                def add(i, sums):
                    return tuple(s + p for s, p in zip(sums, patch(i)))

                found.append(lax.fori_loop(start_ref[d] + 1, start_ref[d + 1], add, patch(start_ref[d])))
            place = pl.ds(pl.multiple_of(group * 8, 8), 8)
            for tile in range(chunk // LANES):
                here = slice(part * chunk + tile * LANES, part * chunk + (tile + 1) * LANES)
                mine = slice(tile * channels, (tile + 1) * channels)
                power = None
                for j, (x, t) in enumerate(parts):
                    s = jnp.concatenate([f[j][mine] for f in found], axis=0)
                    model_ref[x, t, place, here] = s
                    power = s * s if power is None else power + s * s
                validity = valid_ref[:, here].astype(F32)
                power_ref[place, here] = power * jnp.concatenate([validity] * fold, axis=0)


def prepare(cluster, patches, valid, total):
    channels, baselines = valid.shape
    lead = patches.shape[:3]
    tiled = patches.reshape(*lead, channels, baselines // LANES, LANES)
    tiled = jnp.swapaxes(tiled, 3, 4).reshape(*lead, channels * baselines // LANES, LANES)
    chunk = min(PREP_CHUNK, baselines)
    per = DIRECTIONS * channels
    vmem = pl.BlockSpec(memory_space=pltpu.VMEM)
    return pl.pallas_call(
        partial(prep_kernel, total, channels, chunk),
        in_specs=[
            pl.BlockSpec(memory_space=pltpu.HBM),
            pl.BlockSpec(memory_space=pltpu.HBM),
            pl.BlockSpec(memory_space=pltpu.HBM),
        ],
        out_specs=[vmem] * 5,
        out_shape=[
            jax.ShapeDtypeStruct((2, TIME_SLOTS, per, baselines), F32),
            jax.ShapeDtypeStruct((per, baselines), F32),
            jax.ShapeDtypeStruct((10 * HALF, per), F32),
            jax.ShapeDtypeStruct((6 * HALF, per), F32),
            jax.ShapeDtypeStruct((2 * per, 12 * HALF), F32),
        ],
        scratch_shapes=[
            pltpu.VMEM(tiled.shape, BF16),
            pltpu.VMEM(valid.shape, valid.dtype),
            pltpu.SMEM((SKY_PATCHES,), jnp.int32),
            pltpu.SemaphoreType.DMA((baselines // chunk + 2,)),
            pltpu.SMEM((SKY_PATCHES,), jnp.int32),
            pltpu.SMEM((2 * DIRECTIONS + 1,), jnp.int32),
        ],
        compiler_params=pltpu.CompilerParams(vmem_limit_bytes=32 << 20),
        name="prepare",
    )(*(pltpu.with_memory_space_constraint(v, pltpu.HBM) for v in (cluster, tiled, valid)))


def fitted_values(fit_ref, own_ref, other_ref):
    coefs = jnp.concatenate([own_ref[...], other_ref[...]], axis=0)
    return jnp.dot(fit_ref[...], coefs, precision=HIGHEST, preferred_element_type=F32)


def station_sums(picks_ref, terms_ref, rows, columns):
    return lax.dot_general(
        picks_ref[rows, columns], terms_ref[:, columns], (((1,), (1,)), ((), ())), preferred_element_type=F32
    )


def moments(sums, current, normal_ref, right_ref, blocks, own_ref, other_ref):
    per = current.shape[0] // 2
    sums = sums.T
    weight = sums[2 * per:3 * per, :] + 1.0 / blocks
    product = partial(jnp.dot, precision=HIGHEST, preferred_element_type=F32)
    normal = product(normal_ref[...], weight)
    right = [
        product(right_ref[...], weight * current[x * per:(x + 1) * per, :] + sums[x * per:(x + 1) * per, :])
        for x in range(2)
    ]
    for half, out in enumerate((own_ref, other_ref)):
        out[0:5 * HALF, :] = normal[half * 5 * HALF:(half + 1) * 5 * HALF, :]
        for x in range(2):
            out[(5 + 3 * x) * HALF:(8 + 3 * x) * HALF, :] = right[x][half * 3 * HALF:(half + 1) * 3 * HALF, :]


def sweep_kernel(first, blocks, owned, tile, *refs):
    if first:
        gain_refs, refs = refs[:blocks], refs[blocks:]
        (stations_ref, model_ref, power_ref, valid_ref, visible_ref, normal_ref, right_ref,
         own_ref, other_ref, current_ref, terms_ref, picks_ref, *refs) = refs
    else:
        (before_ref, fit_ref, own_coef_ref, other_coef_ref, picks_ref), refs = refs[:5], refs[5:]
        (model_ref, power_ref, valid_ref, visible_ref, normal_ref, right_ref,
         own_ref, other_ref, current_ref, terms_ref, *refs) = refs
    rounded_ref, sums_ref, chosen_ref, ids_ref = refs
    if first:
        ids_ref[...] = iotas(ids_ref.shape)[0].astype(F32).astype(BF16)
    channels, baselines = valid_ref.shape
    per = DIRECTIONS * channels
    stations = blocks * owned
    fold = 8 // channels
    if first:
        for k in range(blocks):
            for x in range(2):
                for d in range(0, DIRECTIONS, fold):
                    row = x * per + d * channels
                    pair = jnp.concatenate([gain_refs[k][x, d + j] for j in range(fold)], axis=0)
                    current_ref[row:row + 8, k * owned:(k + 1) * owned] = pair
    else:
        fitted = fitted_values(fit_ref, own_coef_ref, other_coef_ref)
        current_ref[...] = 0.5 * (before_ref[...] + fitted)
    rounded_ref[...] = current_ref[...].astype(BF16)

    def span(i, width):
        if isinstance(i, int):
            return slice(i * width, (i + 1) * width)
        return pl.ds(pl.multiple_of(i * width, width), width)

    def choose(i):
        here = span(i, 2 * tile)
        if first:
            shift = lax.axis_index("bl") * owned
            place = stations_ref[:, span(i, tile)] - shift
            place = jnp.where(place < 0, place + stations, place)
            columns = []
            for part in range(tile // LANES):
                columns += [place[k:k + 1, part * LANES:(part + 1) * LANES] for k in range(2)]
            place = jnp.concatenate(columns, axis=1)
            ids = ids_ref[...]
            for start in range(0, stations, EXACT):
                local = jnp.where((place >= start) & (place < start + EXACT), place - start, -1)
                local = local.astype(F32).astype(BF16)
                picks_ref[start:start + EXACT, here] = jnp.where(ids == local, jnp.ones((), BF16), jnp.zeros((), BF16))
        chosen_ref[...] = jnp.dot(rounded_ref[...], picks_ref[:, here], preferred_element_type=F32)

    def terms(i):
        for part in range(tile // LANES):
            near, far = (slice((2 * part + k) * LANES, (2 * part + k + 1) * LANES) for k in range(2))
            if isinstance(i, int):
                along = slice(i * tile + part * LANES, i * tile + (part + 1) * LANES)
            else:
                along = pl.ds(pl.multiple_of(i * tile + part * LANES, LANES), LANES)
            pred = [jnp.zeros((8, LANES), F32) for _ in range(2 * TIME_SLOTS)]
            for row in range(0, per, 8):
                re, im = slice(row, row + 8), slice(per + row, per + row + 8)
                pr, pi, qr, qi = chosen_ref[re, near], chosen_ref[im, near], chosen_ref[re, far], chosen_ref[im, far]
                gr = pr * qr + pi * qi
                gi = pi * qr - pr * qi
                for t in range(TIME_SLOTS):
                    mr, mi = model_ref[0, t, re, along], model_ref[1, t, re, along]
                    pred[2 * t] = pred[2 * t] + (gr * mr - gi * mi)
                    pred[2 * t + 1] = pred[2 * t + 1] + (gr * mi + gi * mr)
            validity = valid_ref[:, along].astype(F32)
            resid = []
            for t in range(TIME_SLOTS):
                for x in range(2):
                    p = pred[2 * t + x]
                    total = p[0:channels]
                    for k in range(1, fold):
                        total = total + p[k * channels:(k + 1) * channels]
                    r = (visible_ref[x, t, :, along] - total) * validity
                    resid.append(jnp.concatenate([r] * fold, axis=0))
            rows = [[None] * (per // 8) for _ in range(6)]
            for row in range(0, per, 8):
                re, im = slice(row, row + 8), slice(per + row, per + row + 8)
                pr, pi, qr, qi = chosen_ref[re, near], chosen_ref[im, near], chosen_ref[re, far], chosen_ref[im, far]
                ar = ai = None
                for t in range(TIME_SLOTS):
                    mr, mi = model_ref[0, t, re, along], model_ref[1, t, re, along]
                    rr, ri = resid[2 * t], resid[2 * t + 1]
                    br = mr * rr + mi * ri
                    bi = mr * ri - mi * rr
                    ar, ai = (br, bi) if ar is None else (ar + br, ai + bi)
                power = power_ref[re, along]
                values = (qr * ar - qi * ai, qr * ai + qi * ar, power * (qr * qr + qi * qi),
                          pr * ar + pi * ai, pi * ar - pr * ai, power * (pr * pr + pi * pi))
                for k in range(6):
                    rows[k][row // 8] = values[k]
                if row % 16 == 8:
                    for k in range(6):
                        two = jnp.concatenate(rows[k][row // 8 - 1:row // 8 + 1], axis=0).astype(BF16)
                        place = (k % 3) * per + row - 8
                        column = (2 * (i * (tile // LANES) + part) + k // 3) * LANES
                        if not isinstance(i, int):
                            column = pl.multiple_of(column, LANES)
                        terms_ref[place:place + 16, pl.ds(column, LANES)] = two

    def add_up(i):
        more = station_sums(picks_ref, terms_ref, slice(owned, stations), span(i, 2 * tile))
        if isinstance(i, int) and i == 0:
            sums_ref[...] = more
        else:
            sums_ref[...] += more

    count = baselines // tile
    choose(0)
    terms(0)
    choose(1)
    add_up(0)
    terms(1)
    choose(2)

    @pl.loop(3, count)
    def _(i):
        add_up(i - 2)
        terms(i - 1)
        choose(i)

    add_up(count - 2)
    terms(count - 1)
    add_up(count - 1)

    moments(sums_ref[...], current_ref[:, owned:stations], normal_ref, right_ref, blocks, own_ref, other_ref)


def own_kernel(blocks, chunk, picks_ref, terms_ref, current_ref, normal_ref, right_ref, own_ref, other_ref):
    owned = own_ref.shape[1]
    sums = None
    for start in range(0, picks_ref.shape[1], chunk):
        more = station_sums(picks_ref, terms_ref, slice(0, owned), slice(start, start + chunk))
        sums = more if sums is None else sums + more
    moments(sums, current_ref[:, 0:owned], normal_ref, right_ref, blocks, own_ref, other_ref)


def own_moments(picks, terms, current, normal, right, owned, blocks):
    vmem = pl.BlockSpec(memory_space=pltpu.VMEM)
    return pl.pallas_call(
        partial(own_kernel, blocks, OWN_CHUNK),
        in_specs=[vmem] * 5,
        out_specs=[vmem] * 2,
        out_shape=[jax.ShapeDtypeStruct((11 * HALF, owned), F32)] * 2,
        compiler_params=pltpu.CompilerParams(vmem_limit_bytes=16 << 20),
        cost_estimate=pl.CostEstimate(
            flops=2 * owned * picks.shape[1] * terms.shape[0], transcendentals=0,
            bytes_accessed=2 * picks.shape[1] * (owned + terms.shape[0]),
        ),
        name="own_moments",
    )(picks, terms, current, normal, right)


def sweep(first, inputs, model, power, valid, visible, normal, right, owned, blocks):
    channels, baselines = valid.shape
    per = DIRECTIONS * channels
    count = owned * blocks
    vmem = pl.BlockSpec(memory_space=pltpu.VMEM)
    outs = [
        jax.ShapeDtypeStruct((11 * HALF, count - owned), F32),
        jax.ShapeDtypeStruct((11 * HALF, count - owned), F32),
        jax.ShapeDtypeStruct((2 * per, count), F32),
        jax.ShapeDtypeStruct((3 * per, 2 * baselines), BF16),
    ]
    if first:
        outs.append(jax.ShapeDtypeStruct((count, 2 * baselines), BF16))
    return pl.pallas_call(
        partial(sweep_kernel, first, blocks, owned, SWEEP_TILE),
        in_specs=[vmem] * (len(inputs) + 6),
        out_specs=[vmem] * len(outs),
        out_shape=outs,
        scratch_shapes=[
            pltpu.VMEM((2 * per, count), BF16),
            pltpu.VMEM((count - owned, 3 * per), F32),
            pltpu.VMEM((2 * per, 2 * SWEEP_TILE), F32),
            pltpu.VMEM((EXACT, 2 * SWEEP_TILE), BF16),
        ],
        compiler_params=pltpu.CompilerParams(vmem_limit_bytes=24 << 20),
        name="sweep",
    )(*inputs, model, power, valid, visible, normal, right)


def final_kernel(channels, before_ref, fit_ref, own_ref, other_ref, out_ref):
    per = DIRECTIONS * channels
    result = 0.5 * (before_ref[:, 0:out_ref.shape[3]] + fitted_values(fit_ref, own_ref, other_ref))
    for x in range(2):
        for d in range(DIRECTIONS):
            row = x * per + d * channels
            out_ref[x, d] = result[row:row + channels, :]


def finish(before, fit, own, other, channels):
    owned = own.shape[1]
    return pl.pallas_call(
        partial(final_kernel, channels),
        in_specs=[pl.BlockSpec(memory_space=pltpu.VMEM)] * 4,
        out_specs=pl.BlockSpec(memory_space=pltpu.VMEM),
        out_shape=jax.ShapeDtypeStruct((2, DIRECTIONS, channels, owned), F32),
        compiler_params=pltpu.CompilerParams(vmem_limit_bytes=8 << 20),
        name="finish",
    )(before, fit, own, other)


def solve(moments):
    m = [moments[k * HALF:(k + 1) * HALF] for k in range(11)]
    m.insert(3, 0.5 * (m[0] + m[2]))
    low_aa = jnp.sqrt(m[0])
    low_ba = m[1] / low_aa
    low_ca = m[2] / low_aa
    low_bb = jnp.sqrt(m[3] - low_ba * low_ba)
    low_cb = (m[4] - low_ca * low_ba) / low_bb
    low_cc = jnp.sqrt(m[5] - low_ca * low_ca - low_cb * low_cb)
    out = []
    for x in range(2):
        r = m[6 + 3 * x:9 + 3 * x]
        first_y = r[0] / low_aa
        second_y = (r[1] - low_ba * first_y) / low_bb
        third_y = (r[2] - low_ca * first_y - low_cb * second_y) / low_cc
        third_x = third_y / low_cc
        second_x = (second_y - low_cb * third_x) / low_bb
        first_x = (first_y - low_ba * second_x - low_ca * third_x) / low_aa
        out += [first_x, second_x, third_x]
    return jnp.concatenate(out, axis=0)


def other_core(value):
    count = lax.axis_size("chan")
    return lax.ppermute(value, "chan", [(j, j ^ 1) for j in range(count)])


def from_later(value, k):
    count = lax.axis_size("bl")
    return lax.ppermute(value, "bl", [((j + k) % count, j) for j in range(count)])


def over_chips(value):
    count = lax.axis_size("chan")
    chips = count // 2
    swap = lambda v, k: lax.ppermute(v, "chan", [(j, j ^ (2 * k)) for j in range(count)])
    if chips <= 4:
        parts = [swap(value, k) for k in range(1, chips)]
        for part in parts:
            value = value + part
        return value
    k = 1
    while k < chips:
        value = value + swap(value, k)
        k *= 2
    return value


def body(patches, visibilities, valid, baseline_stations, cluster, gains):
    channels = visibilities.shape[2]
    owned = gains.shape[3]
    blocks = lax.axis_size("bl")
    total = channels * lax.axis_size("chan")
    all_gains = [gains] + [from_later(gains, k) for k in range(1, blocks)]
    model, power, normal, right, fit = prepare(cluster[:, 0], patches, valid, total)
    common = (model, power, valid, visibilities, normal, right, owned, blocks)
    inputs = all_gains + [baseline_stations]
    picks = None
    for number in range(ITERS):
        own, other, current, terms, *made = sweep(number == 0, inputs, *common)
        picks = made[0] if made else picks
        others = own + other_core(other)
        others, terms = lax.optimization_barrier((others, terms))
        received = [
            from_later(others[:, (blocks - k - 1) * owned:(blocks - k) * owned], k) for k in range(1, blocks)
        ]
        own, other = own_moments(picks, terms, current, normal, right, owned, blocks)
        kept = own
        for part in received:
            kept = kept + part
        kept = lax.optimization_barrier(kept) + other_core(other)
        coefs = solve(over_chips(kept))
        if number < ITERS - 1:
            coefs = jnp.concatenate([coefs] + [from_later(coefs, k) for k in range(1, blocks)], axis=1)
        inputs = [current, fit, coefs, other_core(coefs), picks]
    return finish(*inputs[:4], channels)


def solution(mesh):
    in_specs = (
        P(None, None, None, ("grp", "chan"), "bl"),
        P(None, None, ("grp", "chan"), "bl"),
        P(("grp", "chan"), "bl"),
        P(None, "bl"),
        P(),
        P(None, None, ("grp", "chan"), "bl"),
    )
    out_specs = P(None, None, ("grp", "chan"), "bl")
    return jax.shard_map(body, mesh=mesh, in_specs=in_specs, out_specs=out_specs, check_vma=False)
```

```python
from functools import partial

import jax
import jax.numpy as jnp
from jax import lax
from jax.experimental import pallas as pl
from jax.experimental.pallas import tpu as pltpu
from jax.sharding import PartitionSpec as P

DIRECTIONS = 16
SKY_PATCHES = 32
TIME_SLOTS = 2
ITERS = 2
LANES = 128
EXACT = 256
PREP_CHUNK = 1024
SWEEP_TILE = 1024
OWN_CHUNK = 2048
HALF = DIRECTIONS // 2
HIGHEST = lax.Precision.HIGHEST
F32, BF16 = jnp.float32, jnp.bfloat16


def basis_at(channel, total):
    ratio = 1.0 + channel.astype(F32) / total
    inverse = 4.0 / ratio - 3.0
    return jnp.ones_like(inverse), inverse, 2.0 * inverse * inverse - 1.0


def iotas(shape):
    return lax.broadcasted_iota(jnp.int32, shape, 0), lax.broadcasted_iota(jnp.int32, shape, 1)


def pick(index, values):
    out = values[-1]
    for k in range(len(values) - 2, -1, -1):
        out = jnp.where(index == k, values[k], out)
    return out


def moment_matrix(terms, channels, total, chan):
    row, col = iotas((2 * terms * HALF, DIRECTIONS * channels))
    block = row // HALF
    half = (block >= terms).astype(jnp.int32)
    term = block - half * terms
    direction = jnp.bitwise_xor(half, lax.rem(chan, 2)) * HALF + row % HALF
    one, first, second = basis_at(chan * channels + col % channels, total)
    if terms == 5:
        values = (one, first, second, first * second, second * second)
    else:
        values = (one, first, second)
    return jnp.where(direction == col // channels, pick(term, values), 0.0)


def fit_matrix(channels, total, chan):
    per = DIRECTIONS * channels
    row, col = iotas((2 * per, 12 * HALF))
    place = row % per
    block = col // HALF
    half = (block >= 6).astype(jnp.int32)
    block = block - 6 * half
    direction = jnp.bitwise_xor(half, lax.rem(chan, 2)) * HALF + col % HALF
    basis = basis_at(chan * channels + place % channels, total)
    same = (direction == place // channels) & (row // per == block // 3)
    return jnp.where(same, pick(block % 3, basis), 0.0)


def prep_kernel(total, channels, chunk, cluster_hbm, patches_hbm, valid_hbm, model_ref, power_ref,
                normal_ref, right_ref, fit_ref, patches_ref, valid_ref, cluster_ref, sems, order_ref, start_ref):
    chan = lax.axis_index("chan")
    baselines = valid_ref.shape[1]
    cluster_copy = pltpu.make_async_copy(cluster_hbm, cluster_ref, sems.at[baselines // chunk])
    cluster_copy.start()
    valid_copy = pltpu.make_async_copy(valid_hbm, valid_ref, sems.at[baselines // chunk + 1])
    valid_copy.start()
    copies = []
    rows = channels * chunk // LANES
    for part in range(baselines // chunk):
        here = pl.ds(part * rows, rows)
        copies.append(pltpu.make_async_copy(patches_hbm.at[:, :, :, here], patches_ref.at[:, :, :, here], sems.at[part]))
        copies[-1].start()
    normal_ref[...] = moment_matrix(5, channels, total, chan)
    right_ref[...] = moment_matrix(3, channels, total, chan)
    fit_ref[...] = fit_matrix(channels, total, chan)
    for d in range(DIRECTIONS + 1):
        start_ref[d] = 0
    cluster_copy.wait()

    @pl.loop(0, SKY_PATCHES)
    def _(q):
        d = cluster_ref[q]
        start_ref[d + 1] = start_ref[d + 1] + 1

    for d in range(DIRECTIONS):
        start_ref[d + 1] = start_ref[d + 1] + start_ref[d]
    for d in range(DIRECTIONS):
        start_ref[DIRECTIONS + 1 + d] = start_ref[d]

    @pl.loop(0, SKY_PATCHES)
    def _(q):
        d = cluster_ref[q]
        place = start_ref[DIRECTIONS + 1 + d]
        order_ref[place] = q
        start_ref[DIRECTIONS + 1 + d] = place + 1

    valid_copy.wait()
    fold = 8 // channels
    parts = [(x, t) for x in range(2) for t in range(TIME_SLOTS)]
    for part in range(baselines // chunk):
        copies[part].wait()
        own_rows = slice(part * rows, (part + 1) * rows)

        @pl.loop(0, DIRECTIONS // fold)
        def _(group):
            found = []
            for k in range(fold):
                d = group * fold + k

                def patch(i):
                    q = order_ref[i]
                    return tuple(patches_ref[q, x, t, own_rows, :].astype(F32) for x, t in parts)

                def add(i, sums):
                    return tuple(s + p for s, p in zip(sums, patch(i)))

                found.append(lax.fori_loop(start_ref[d] + 1, start_ref[d + 1], add, patch(start_ref[d])))
            place = pl.ds(pl.multiple_of(group * 8, 8), 8)
            for tile in range(chunk // LANES):
                here = slice(part * chunk + tile * LANES, part * chunk + (tile + 1) * LANES)
                mine = slice(tile * channels, (tile + 1) * channels)
                power = None
                for j, (x, t) in enumerate(parts):
                    s = jnp.concatenate([f[j][mine] for f in found], axis=0)
                    model_ref[x, t, place, here] = s
                    power = s * s if power is None else power + s * s
                validity = valid_ref[:, here].astype(F32)
                power_ref[place, here] = power * jnp.concatenate([validity] * fold, axis=0)


def prepare(cluster, patches, valid, total):
    channels, baselines = valid.shape
    lead = patches.shape[:3]
    tiled = patches.reshape(*lead, channels, baselines // LANES, LANES)
    tiled = jnp.swapaxes(tiled, 3, 4).reshape(*lead, channels * baselines // LANES, LANES)
    chunk = min(PREP_CHUNK, baselines)
    per = DIRECTIONS * channels
    vmem = pl.BlockSpec(memory_space=pltpu.VMEM)
    return pl.pallas_call(
        partial(prep_kernel, total, channels, chunk),
        in_specs=[
            pl.BlockSpec(memory_space=pltpu.HBM),
            pl.BlockSpec(memory_space=pltpu.HBM),
            pl.BlockSpec(memory_space=pltpu.HBM),
        ],
        out_specs=[vmem] * 5,
        out_shape=[
            jax.ShapeDtypeStruct((2, TIME_SLOTS, per, baselines), F32),
            jax.ShapeDtypeStruct((per, baselines), F32),
            jax.ShapeDtypeStruct((10 * HALF, per), F32),
            jax.ShapeDtypeStruct((6 * HALF, per), F32),
            jax.ShapeDtypeStruct((2 * per, 12 * HALF), F32),
        ],
        scratch_shapes=[
            pltpu.VMEM(tiled.shape, BF16),
            pltpu.VMEM(valid.shape, valid.dtype),
            pltpu.SMEM((SKY_PATCHES,), jnp.int32),
            pltpu.SemaphoreType.DMA((baselines // chunk + 2,)),
            pltpu.SMEM((SKY_PATCHES,), jnp.int32),
            pltpu.SMEM((2 * DIRECTIONS + 1,), jnp.int32),
        ],
        compiler_params=pltpu.CompilerParams(vmem_limit_bytes=32 << 20),
        name="prepare",
    )(*(pltpu.with_memory_space_constraint(v, pltpu.HBM) for v in (cluster, tiled, valid)))


def fitted_values(fit_ref, own_ref, other_ref):
    coefs = jnp.concatenate([own_ref[...], other_ref[...]], axis=0)
    return jnp.dot(fit_ref[...], coefs, precision=HIGHEST, preferred_element_type=F32)


def station_sums(picks_ref, terms_ref, rows, columns):
    return lax.dot_general(
        picks_ref[rows, columns], terms_ref[:, columns], (((1,), (1,)), ((), ())), preferred_element_type=F32
    )


def moments(sums, current, normal_ref, right_ref, blocks, own_ref, other_ref):
    per = current.shape[0] // 2
    sums = sums.T
    weight = sums[2 * per:3 * per, :] + 1.0 / blocks
    product = partial(jnp.dot, precision=HIGHEST, preferred_element_type=F32)
    normal = product(normal_ref[...], weight)
    right = [
        product(right_ref[...], weight * current[x * per:(x + 1) * per, :] + sums[x * per:(x + 1) * per, :])
        for x in range(2)
    ]
    for half, out in enumerate((own_ref, other_ref)):
        out[0:5 * HALF, :] = normal[half * 5 * HALF:(half + 1) * 5 * HALF, :]
        for x in range(2):
            out[(5 + 3 * x) * HALF:(8 + 3 * x) * HALF, :] = right[x][half * 3 * HALF:(half + 1) * 3 * HALF, :]


def sweep_kernel(first, blocks, owned, tile, *refs):
    if first:
        gain_refs, refs = refs[:blocks], refs[blocks:]
        (stations_ref, model_ref, power_ref, valid_ref, visible_ref, normal_ref, right_ref,
         own_ref, other_ref, current_ref, terms_ref, picks_ref, *refs) = refs
    else:
        (before_ref, fit_ref, own_coef_ref, other_coef_ref, picks_ref), refs = refs[:5], refs[5:]
        (model_ref, power_ref, valid_ref, visible_ref, normal_ref, right_ref,
         own_ref, other_ref, current_ref, terms_ref, *refs) = refs
    rounded_ref, sums_ref, chosen_ref, ids_ref = refs
    if first:
        ids_ref[...] = iotas(ids_ref.shape)[0].astype(F32).astype(BF16)
    channels, baselines = valid_ref.shape
    per = DIRECTIONS * channels
    stations = blocks * owned
    fold = 8 // channels
    if first:
        for k in range(blocks):
            for x in range(2):
                for d in range(0, DIRECTIONS, fold):
                    row = x * per + d * channels
                    pair = jnp.concatenate([gain_refs[k][x, d + j] for j in range(fold)], axis=0)
                    current_ref[row:row + 8, k * owned:(k + 1) * owned] = pair
    else:
        fitted = fitted_values(fit_ref, own_coef_ref, other_coef_ref)
        current_ref[...] = 0.5 * (before_ref[...] + fitted)
    rounded_ref[...] = current_ref[...].astype(BF16)

    def span(i, width):
        if isinstance(i, int):
            return slice(i * width, (i + 1) * width)
        return pl.ds(pl.multiple_of(i * width, width), width)

    def choose(i):
        here = span(i, 2 * tile)
        if first:
            shift = lax.axis_index("bl") * owned
            place = stations_ref[:, span(i, tile)] - shift
            place = jnp.where(place < 0, place + stations, place)
            columns = []
            for part in range(tile // LANES):
                columns += [place[k:k + 1, part * LANES:(part + 1) * LANES] for k in range(2)]
            place = jnp.concatenate(columns, axis=1)
            ids = ids_ref[...]
            for start in range(0, stations, EXACT):
                local = jnp.where((place >= start) & (place < start + EXACT), place - start, -1)
                local = local.astype(F32).astype(BF16)
                picks_ref[start:start + EXACT, here] = jnp.where(ids == local, jnp.ones((), BF16), jnp.zeros((), BF16))
        chosen_ref[...] = jnp.dot(rounded_ref[...], picks_ref[:, here], preferred_element_type=F32)

    def terms(i):
        for part in range(tile // LANES):
            near, far = (slice((2 * part + k) * LANES, (2 * part + k + 1) * LANES) for k in range(2))
            if isinstance(i, int):
                along = slice(i * tile + part * LANES, i * tile + (part + 1) * LANES)
            else:
                along = pl.ds(pl.multiple_of(i * tile + part * LANES, LANES), LANES)
            pred = [jnp.zeros((8, LANES), F32) for _ in range(2 * TIME_SLOTS)]
            for row in range(0, per, 8):
                re, im = slice(row, row + 8), slice(per + row, per + row + 8)
                pr, pi, qr, qi = chosen_ref[re, near], chosen_ref[im, near], chosen_ref[re, far], chosen_ref[im, far]
                gr = pr * qr + pi * qi
                gi = pi * qr - pr * qi
                for t in range(TIME_SLOTS):
                    mr, mi = model_ref[0, t, re, along], model_ref[1, t, re, along]
                    pred[2 * t] = pred[2 * t] + (gr * mr - gi * mi)
                    pred[2 * t + 1] = pred[2 * t + 1] + (gr * mi + gi * mr)
            validity = valid_ref[:, along].astype(F32)
            resid = []
            for t in range(TIME_SLOTS):
                for x in range(2):
                    p = pred[2 * t + x]
                    total = p[0:channels]
                    for k in range(1, fold):
                        total = total + p[k * channels:(k + 1) * channels]
                    r = (visible_ref[x, t, :, along] - total) * validity
                    resid.append(jnp.concatenate([r] * fold, axis=0))
            rows = [[None] * (per // 8) for _ in range(6)]
            for row in range(0, per, 8):
                re, im = slice(row, row + 8), slice(per + row, per + row + 8)
                pr, pi, qr, qi = chosen_ref[re, near], chosen_ref[im, near], chosen_ref[re, far], chosen_ref[im, far]
                ar = ai = None
                for t in range(TIME_SLOTS):
                    mr, mi = model_ref[0, t, re, along], model_ref[1, t, re, along]
                    rr, ri = resid[2 * t], resid[2 * t + 1]
                    br = mr * rr + mi * ri
                    bi = mr * ri - mi * rr
                    ar, ai = (br, bi) if ar is None else (ar + br, ai + bi)
                power = power_ref[re, along]
                values = (qr * ar - qi * ai, qr * ai + qi * ar, power * (qr * qr + qi * qi),
                          pr * ar + pi * ai, pi * ar - pr * ai, power * (pr * pr + pi * pi))
                for k in range(6):
                    rows[k][row // 8] = values[k]
                if row % 16 == 8:
                    for k in range(6):
                        two = jnp.concatenate(rows[k][row // 8 - 1:row // 8 + 1], axis=0).astype(BF16)
                        place = (k % 3) * per + row - 8
                        column = (2 * (i * (tile // LANES) + part) + k // 3) * LANES
                        if not isinstance(i, int):
                            column = pl.multiple_of(column, LANES)
                        terms_ref[place:place + 16, pl.ds(column, LANES)] = two

    def add_up(i):
        more = station_sums(picks_ref, terms_ref, slice(owned, stations), span(i, 2 * tile))
        if isinstance(i, int) and i == 0:
            sums_ref[...] = more
        else:
            sums_ref[...] += more

    count = baselines // tile
    choose(0)
    terms(0)
    choose(1)
    add_up(0)
    terms(1)
    choose(2)

    @pl.loop(3, count)
    def _(i):
        add_up(i - 2)
        terms(i - 1)
        choose(i)

    add_up(count - 2)
    terms(count - 1)
    add_up(count - 1)

    moments(sums_ref[...], current_ref[:, owned:stations], normal_ref, right_ref, blocks, own_ref, other_ref)


def own_kernel(blocks, chunk, picks_ref, terms_ref, current_ref, normal_ref, right_ref, own_ref, other_ref):
    owned = own_ref.shape[1]
    sums = None
    for start in range(0, picks_ref.shape[1], chunk):
        more = station_sums(picks_ref, terms_ref, slice(0, owned), slice(start, start + chunk))
        sums = more if sums is None else sums + more
    moments(sums, current_ref[:, 0:owned], normal_ref, right_ref, blocks, own_ref, other_ref)


def own_moments(picks, terms, current, normal, right, owned, blocks):
    vmem = pl.BlockSpec(memory_space=pltpu.VMEM)
    return pl.pallas_call(
        partial(own_kernel, blocks, OWN_CHUNK),
        in_specs=[vmem] * 5,
        out_specs=[vmem] * 2,
        out_shape=[jax.ShapeDtypeStruct((11 * HALF, owned), F32)] * 2,
        compiler_params=pltpu.CompilerParams(vmem_limit_bytes=16 << 20),
        cost_estimate=pl.CostEstimate(
            flops=2 * owned * picks.shape[1] * terms.shape[0], transcendentals=0,
            bytes_accessed=2 * picks.shape[1] * (owned + terms.shape[0]),
        ),
        name="own_moments",
    )(picks, terms, current, normal, right)


def sweep(first, inputs, model, power, valid, visible, normal, right, owned, blocks):
    channels, baselines = valid.shape
    per = DIRECTIONS * channels
    count = owned * blocks
    vmem = pl.BlockSpec(memory_space=pltpu.VMEM)
    outs = [
        jax.ShapeDtypeStruct((11 * HALF, count - owned), F32),
        jax.ShapeDtypeStruct((11 * HALF, count - owned), F32),
        jax.ShapeDtypeStruct((2 * per, count), F32),
        jax.ShapeDtypeStruct((3 * per, 2 * baselines), BF16),
    ]
    if first:
        outs.append(jax.ShapeDtypeStruct((count, 2 * baselines), BF16))
    return pl.pallas_call(
        partial(sweep_kernel, first, blocks, owned, SWEEP_TILE),
        in_specs=[vmem] * (len(inputs) + 6),
        out_specs=[vmem] * len(outs),
        out_shape=outs,
        scratch_shapes=[
            pltpu.VMEM((2 * per, count), BF16),
            pltpu.VMEM((count - owned, 3 * per), F32),
            pltpu.VMEM((2 * per, 2 * SWEEP_TILE), F32),
            pltpu.VMEM((EXACT, 2 * SWEEP_TILE), BF16),
        ],
        compiler_params=pltpu.CompilerParams(vmem_limit_bytes=24 << 20),
        name="sweep",
    )(*inputs, model, power, valid, visible, normal, right)


def final_kernel(channels, before_ref, fit_ref, own_ref, other_ref, out_ref):
    per = DIRECTIONS * channels
    result = 0.5 * (before_ref[:, 0:out_ref.shape[3]] + fitted_values(fit_ref, own_ref, other_ref))
    for x in range(2):
        for d in range(DIRECTIONS):
            row = x * per + d * channels
            out_ref[x, d] = result[row:row + channels, :]


def finish(before, fit, own, other, channels):
    owned = own.shape[1]
    return pl.pallas_call(
        partial(final_kernel, channels),
        in_specs=[pl.BlockSpec(memory_space=pltpu.VMEM)] * 4,
        out_specs=pl.BlockSpec(memory_space=pltpu.VMEM),
        out_shape=jax.ShapeDtypeStruct((2, DIRECTIONS, channels, owned), F32),
        compiler_params=pltpu.CompilerParams(vmem_limit_bytes=8 << 20),
        name="finish",
    )(before, fit, own, other)


def solve(moments):
    m = [moments[k * HALF:(k + 1) * HALF] for k in range(11)]
    m.insert(3, 0.5 * (m[0] + m[2]))
    low_aa = jnp.sqrt(m[0])
    low_ba = m[1] / low_aa
    low_ca = m[2] / low_aa
    low_bb = jnp.sqrt(m[3] - low_ba * low_ba)
    low_cb = (m[4] - low_ca * low_ba) / low_bb
    low_cc = jnp.sqrt(m[5] - low_ca * low_ca - low_cb * low_cb)
    out = []
    for x in range(2):
        r = m[6 + 3 * x:9 + 3 * x]
        first_y = r[0] / low_aa
        second_y = (r[1] - low_ba * first_y) / low_bb
        third_y = (r[2] - low_ca * first_y - low_cb * second_y) / low_cc
        third_x = third_y / low_cc
        second_x = (second_y - low_cb * third_x) / low_bb
        first_x = (first_y - low_ba * second_x - low_ca * third_x) / low_aa
        out += [first_x, second_x, third_x]
    return jnp.concatenate(out, axis=0)


def other_core(value):
    count = lax.axis_size("chan")
    return lax.ppermute(value, "chan", [(j, j ^ 1) for j in range(count)])


def from_later(value, k, cross=False):
    count = lax.axis_size("bl")
    if not cross:
        return lax.ppermute(value, "bl", [((j + k) % count, j) for j in range(count)])
    pairs = [
        ((c ^ 1) * count + (j + k) % count, c * count + j) for c in range(lax.axis_size("chan")) for j in range(count)
    ]
    return lax.ppermute(value, ("chan", "bl"), pairs)


def over_chips(value):
    count = lax.axis_size("chan")
    chips = count // 2
    swap = lambda v, k: lax.ppermute(v, "chan", [(j, j ^ (2 * k)) for j in range(count)])
    if chips <= 4:
        order = (1, 3, 2) if chips == 4 else range(1, chips)
        parts = [swap(value, k) for k in order]
        for part in parts:
            value = value + part
        return value
    k = 1
    while k < chips:
        value = value + swap(value, k)
        k *= 2
    return value


def body(patches, visibilities, valid, baseline_stations, cluster, gains):
    channels = visibilities.shape[2]
    owned = gains.shape[3]
    blocks = lax.axis_size("bl")
    total = channels * lax.axis_size("chan")
    all_gains = [gains] + [from_later(gains, k) for k in range(1, blocks)]
    model, power, normal, right, fit = prepare(cluster[:, 0], patches, valid, total)
    common = (model, power, valid, visibilities, normal, right, owned, blocks)
    inputs = all_gains + [baseline_stations]
    picks = None
    for number in range(ITERS):
        own, other, current, terms, *made = sweep(number == 0, inputs, *common)
        picks = made[0] if made else picks
        others = own + other_core(other)
        others, terms = lax.optimization_barrier((others, terms))
        received = [
            from_later(others[:, (blocks - k - 1) * owned:(blocks - k) * owned], k) for k in range(1, blocks)
        ]
        own, other = own_moments(picks, terms, current, normal, right, owned, blocks)
        kept = own
        for part in received:
            kept = kept + part
        kept = lax.optimization_barrier(kept) + other_core(other)
        coefs = solve(over_chips(kept))
        if number < ITERS - 1:
            across = [from_later(coefs, k, True) for k in range(1, blocks)]
            along = [from_later(coefs, k) for k in range(1, blocks)]
            beside = other_core(coefs)
            inputs = [current, fit, jnp.concatenate([coefs] + along, axis=1), jnp.concatenate([beside] + across, axis=1), picks]
        else:
            inputs = [current, fit, coefs, other_core(coefs), picks]
    return finish(*inputs[:4], channels)


def solution(mesh):
    in_specs = (
        P(None, None, None, ("grp", "chan"), "bl"),
        P(None, None, ("grp", "chan"), "bl"),
        P(("grp", "chan"), "bl"),
        P(None, "bl"),
        P(),
        P(None, None, ("grp", "chan"), "bl"),
    )
    out_specs = P(None, None, ("grp", "chan"), "bl")
    return jax.shard_map(body, mesh=mesh, in_specs=in_specs, out_specs=out_specs, check_vma=False)
```

```python
from functools import partial

import jax
import jax.numpy as jnp
from jax import lax
from jax.experimental import pallas as pl
from jax.experimental.pallas import tpu as pltpu
from jax.sharding import PartitionSpec as P

DIRECTIONS = 16
SKY_PATCHES = 32
TIME_SLOTS = 2
ITERS = 2
LANES = 128
EXACT = 256
PREP_CHUNK = 1024
SWEEP_TILE = 1024
OWN_CHUNK = 2048
HALF = DIRECTIONS // 2
HIGHEST = lax.Precision.HIGHEST
F32, BF16 = jnp.float32, jnp.bfloat16


def basis_at(channel, total):
    ratio = 1.0 + channel.astype(F32) / total
    inverse = 4.0 / ratio - 3.0
    return jnp.ones_like(inverse), inverse, 2.0 * inverse * inverse - 1.0


def iotas(shape):
    return lax.broadcasted_iota(jnp.int32, shape, 0), lax.broadcasted_iota(jnp.int32, shape, 1)


def pick(index, values):
    out = values[-1]
    for k in range(len(values) - 2, -1, -1):
        out = jnp.where(index == k, values[k], out)
    return out


def moment_matrix(terms, channels, total, chan):
    row, col = iotas((2 * terms * HALF, DIRECTIONS * channels))
    block = row // HALF
    half = (block >= terms).astype(jnp.int32)
    term = block - half * terms
    direction = jnp.bitwise_xor(half, lax.rem(chan, 2)) * HALF + row % HALF
    one, first, second = basis_at(chan * channels + col % channels, total)
    if terms == 5:
        values = (one, first, second, first * second, second * second)
    else:
        values = (one, first, second)
    return jnp.where(direction == col // channels, pick(term, values), 0.0)


def fit_matrix(channels, total, chan):
    per = DIRECTIONS * channels
    row, col = iotas((2 * per, 12 * HALF))
    place = row % per
    block = col // HALF
    half = (block >= 6).astype(jnp.int32)
    block = block - 6 * half
    direction = jnp.bitwise_xor(half, lax.rem(chan, 2)) * HALF + col % HALF
    basis = basis_at(chan * channels + place % channels, total)
    same = (direction == place // channels) & (row // per == block // 3)
    return jnp.where(same, pick(block % 3, basis), 0.0)


def prep_kernel(total, channels, chunk, cluster_hbm, patches_hbm, valid_hbm, model_ref, power_ref,
                normal_ref, right_ref, fit_ref, patches_ref, valid_ref, cluster_ref, sems, order_ref, start_ref):
    chan = lax.axis_index("chan")
    baselines = valid_ref.shape[1]
    cluster_copy = pltpu.make_async_copy(cluster_hbm, cluster_ref, sems.at[baselines // chunk])
    cluster_copy.start()
    valid_copy = pltpu.make_async_copy(valid_hbm, valid_ref, sems.at[baselines // chunk + 1])
    valid_copy.start()
    copies = []
    rows = channels * chunk // LANES
    for part in range(baselines // chunk):
        here = pl.ds(part * rows, rows)
        copies.append(pltpu.make_async_copy(patches_hbm.at[:, :, :, here], patches_ref.at[:, :, :, here], sems.at[part]))
        copies[-1].start()
    normal_ref[...] = moment_matrix(5, channels, total, chan)
    right_ref[...] = moment_matrix(3, channels, total, chan)
    fit_ref[...] = fit_matrix(channels, total, chan)
    for d in range(DIRECTIONS + 1):
        start_ref[d] = 0
    cluster_copy.wait()

    @pl.loop(0, SKY_PATCHES)
    def _(q):
        d = cluster_ref[q]
        start_ref[d + 1] = start_ref[d + 1] + 1

    for d in range(DIRECTIONS):
        start_ref[d + 1] = start_ref[d + 1] + start_ref[d]
    for d in range(DIRECTIONS):
        start_ref[DIRECTIONS + 1 + d] = start_ref[d]

    @pl.loop(0, SKY_PATCHES)
    def _(q):
        d = cluster_ref[q]
        place = start_ref[DIRECTIONS + 1 + d]
        order_ref[place] = q
        start_ref[DIRECTIONS + 1 + d] = place + 1

    valid_copy.wait()
    fold = 8 // channels
    parts = [(x, t) for x in range(2) for t in range(TIME_SLOTS)]
    for part in range(baselines // chunk):
        copies[part].wait()
        own_rows = slice(part * rows, (part + 1) * rows)

        @pl.loop(0, DIRECTIONS // fold)
        def _(group):
            found = []
            for k in range(fold):
                d = group * fold + k

                def patch(i):
                    q = order_ref[i]
                    return tuple(patches_ref[q, x, t, own_rows, :].astype(F32) for x, t in parts)

                def add(i, sums):
                    return tuple(s + p for s, p in zip(sums, patch(i)))

                found.append(lax.fori_loop(start_ref[d] + 1, start_ref[d + 1], add, patch(start_ref[d])))
            place = pl.ds(pl.multiple_of(group * 8, 8), 8)
            for tile in range(chunk // LANES):
                here = slice(part * chunk + tile * LANES, part * chunk + (tile + 1) * LANES)
                mine = slice(tile * channels, (tile + 1) * channels)
                power = None
                for j, (x, t) in enumerate(parts):
                    s = jnp.concatenate([f[j][mine] for f in found], axis=0)
                    model_ref[x, t, place, here] = s
                    power = s * s if power is None else power + s * s
                validity = valid_ref[:, here].astype(F32)
                power_ref[place, here] = power * jnp.concatenate([validity] * fold, axis=0)


def prepare(cluster, patches, valid, total):
    channels, baselines = valid.shape
    lead = patches.shape[:3]
    tiled = patches.reshape(*lead, channels, baselines // LANES, LANES)
    tiled = jnp.swapaxes(tiled, 3, 4).reshape(*lead, channels * baselines // LANES, LANES)
    chunk = min(PREP_CHUNK, baselines)
    per = DIRECTIONS * channels
    vmem = pl.BlockSpec(memory_space=pltpu.VMEM)
    return pl.pallas_call(
        partial(prep_kernel, total, channels, chunk),
        in_specs=[
            pl.BlockSpec(memory_space=pltpu.HBM),
            pl.BlockSpec(memory_space=pltpu.HBM),
            pl.BlockSpec(memory_space=pltpu.HBM),
        ],
        out_specs=[vmem] * 5,
        out_shape=[
            jax.ShapeDtypeStruct((2, TIME_SLOTS, per, baselines), F32),
            jax.ShapeDtypeStruct((per, baselines), F32),
            jax.ShapeDtypeStruct((10 * HALF, per), F32),
            jax.ShapeDtypeStruct((6 * HALF, per), F32),
            jax.ShapeDtypeStruct((2 * per, 12 * HALF), F32),
        ],
        scratch_shapes=[
            pltpu.VMEM(tiled.shape, BF16),
            pltpu.VMEM(valid.shape, valid.dtype),
            pltpu.SMEM((SKY_PATCHES,), jnp.int32),
            pltpu.SemaphoreType.DMA((baselines // chunk + 2,)),
            pltpu.SMEM((SKY_PATCHES,), jnp.int32),
            pltpu.SMEM((2 * DIRECTIONS + 1,), jnp.int32),
        ],
        compiler_params=pltpu.CompilerParams(vmem_limit_bytes=32 << 20),
        name="prepare",
    )(*(pltpu.with_memory_space_constraint(v, pltpu.HBM) for v in (cluster, tiled, valid)))


def fitted_values(fit_ref, own_ref, other_ref):
    coefs = jnp.concatenate([own_ref[...], other_ref[...]], axis=0)
    return jnp.dot(fit_ref[...], coefs, precision=HIGHEST, preferred_element_type=F32)


def station_sums(picks_ref, terms_ref, rows, columns):
    return lax.dot_general(
        picks_ref[rows, columns], terms_ref[:, columns], (((1,), (1,)), ((), ())), preferred_element_type=F32
    )


def moments(sums, current, normal_ref, right_ref, blocks, own_ref, other_ref):
    per = current.shape[0] // 2
    sums = sums.T
    weight = sums[2 * per:3 * per, :] + 1.0 / blocks
    product = partial(jnp.dot, precision=HIGHEST, preferred_element_type=F32)
    normal = product(normal_ref[...], weight)
    right = [
        product(right_ref[...], weight * current[x * per:(x + 1) * per, :] + sums[x * per:(x + 1) * per, :])
        for x in range(2)
    ]
    for half, out in enumerate((own_ref, other_ref)):
        out[0:5 * HALF, :] = normal[half * 5 * HALF:(half + 1) * 5 * HALF, :]
        for x in range(2):
            out[(5 + 3 * x) * HALF:(8 + 3 * x) * HALF, :] = right[x][half * 3 * HALF:(half + 1) * 3 * HALF, :]


def sweep_kernel(first, blocks, owned, tile, *refs):
    if first:
        gain_refs, refs = refs[:blocks], refs[blocks:]
        (stations_ref, model_ref, power_ref, valid_ref, visible_ref, normal_ref, right_ref,
         own_ref, other_ref, current_ref, terms_ref, picks_ref, *refs) = refs
    else:
        (before_ref, fit_ref, own_coef_ref, other_coef_ref, picks_ref), refs = refs[:5], refs[5:]
        (model_ref, power_ref, valid_ref, visible_ref, normal_ref, right_ref,
         own_ref, other_ref, current_ref, terms_ref, *refs) = refs
    rounded_ref, sums_ref, chosen_ref, ids_ref = refs
    if first:
        ids_ref[...] = iotas(ids_ref.shape)[0].astype(F32).astype(BF16)
    channels, baselines = valid_ref.shape
    per = DIRECTIONS * channels
    stations = blocks * owned
    fold = 8 // channels
    if first:
        for k in range(blocks):
            for x in range(2):
                for d in range(0, DIRECTIONS, fold):
                    row = x * per + d * channels
                    pair = jnp.concatenate([gain_refs[k][x, d + j] for j in range(fold)], axis=0)
                    current_ref[row:row + 8, k * owned:(k + 1) * owned] = pair
    else:
        fitted = fitted_values(fit_ref, own_coef_ref, other_coef_ref)
        current_ref[...] = 0.5 * (before_ref[...] + fitted)
    rounded_ref[...] = current_ref[...].astype(BF16)

    def span(i, width):
        if isinstance(i, int):
            return slice(i * width, (i + 1) * width)
        return pl.ds(pl.multiple_of(i * width, width), width)

    def choose(i):
        here = span(i, 2 * tile)
        if first:
            shift = lax.axis_index("bl") * owned
            place = stations_ref[:, span(i, tile)] - shift
            place = jnp.where(place < 0, place + stations, place)
            columns = []
            for part in range(tile // LANES):
                columns += [place[k:k + 1, part * LANES:(part + 1) * LANES] for k in range(2)]
            place = jnp.concatenate(columns, axis=1)
            ids = ids_ref[...]
            for start in range(0, stations, EXACT):
                local = jnp.where((place >= start) & (place < start + EXACT), place - start, -1)
                local = local.astype(F32).astype(BF16)
                picks_ref[start:start + EXACT, here] = jnp.where(ids == local, jnp.ones((), BF16), jnp.zeros((), BF16))
        chosen_ref[...] = jnp.dot(rounded_ref[...], picks_ref[:, here], preferred_element_type=F32)

    def terms(i):
        for part in range(tile // LANES):
            near, far = (slice((2 * part + k) * LANES, (2 * part + k + 1) * LANES) for k in range(2))
            if isinstance(i, int):
                along = slice(i * tile + part * LANES, i * tile + (part + 1) * LANES)
            else:
                along = pl.ds(pl.multiple_of(i * tile + part * LANES, LANES), LANES)
            pred = [jnp.zeros((8, LANES), F32) for _ in range(2 * TIME_SLOTS)]
            for row in range(0, per, 8):
                re, im = slice(row, row + 8), slice(per + row, per + row + 8)
                pr, pi, qr, qi = chosen_ref[re, near], chosen_ref[im, near], chosen_ref[re, far], chosen_ref[im, far]
                gr = pr * qr + pi * qi
                gi = pi * qr - pr * qi
                for t in range(TIME_SLOTS):
                    mr, mi = model_ref[0, t, re, along], model_ref[1, t, re, along]
                    pred[2 * t] = pred[2 * t] + (gr * mr - gi * mi)
                    pred[2 * t + 1] = pred[2 * t + 1] + (gr * mi + gi * mr)
            validity = valid_ref[:, along].astype(F32)
            resid = []
            for t in range(TIME_SLOTS):
                for x in range(2):
                    p = pred[2 * t + x]
                    total = p[0:channels]
                    for k in range(1, fold):
                        total = total + p[k * channels:(k + 1) * channels]
                    r = (visible_ref[x, t, :, along] - total) * validity
                    resid.append(jnp.concatenate([r] * fold, axis=0))
            rows = [[None] * (per // 8) for _ in range(6)]
            for row in range(0, per, 8):
                re, im = slice(row, row + 8), slice(per + row, per + row + 8)
                pr, pi, qr, qi = chosen_ref[re, near], chosen_ref[im, near], chosen_ref[re, far], chosen_ref[im, far]
                ar = ai = None
                for t in range(TIME_SLOTS):
                    mr, mi = model_ref[0, t, re, along], model_ref[1, t, re, along]
                    rr, ri = resid[2 * t], resid[2 * t + 1]
                    br = mr * rr + mi * ri
                    bi = mr * ri - mi * rr
                    ar, ai = (br, bi) if ar is None else (ar + br, ai + bi)
                power = power_ref[re, along]
                values = (qr * ar - qi * ai, qr * ai + qi * ar, power * (qr * qr + qi * qi),
                          pr * ar + pi * ai, pi * ar - pr * ai, power * (pr * pr + pi * pi))
                for k in range(6):
                    rows[k][row // 8] = values[k]
                if row % 16 == 8:
                    for k in range(6):
                        two = jnp.concatenate(rows[k][row // 8 - 1:row // 8 + 1], axis=0).astype(BF16)
                        place = (k % 3) * per + row - 8
                        column = (2 * (i * (tile // LANES) + part) + k // 3) * LANES
                        if not isinstance(i, int):
                            column = pl.multiple_of(column, LANES)
                        terms_ref[place:place + 16, pl.ds(column, LANES)] = two

    def add_up(i):
        more = station_sums(picks_ref, terms_ref, slice(owned, stations), span(i, 2 * tile))
        if isinstance(i, int) and i == 0:
            sums_ref[...] = more
        else:
            sums_ref[...] += more

    count = baselines // tile
    choose(0)
    terms(0)
    choose(1)
    add_up(0)
    terms(1)
    choose(2)

    @pl.loop(3, count)
    def _(i):
        add_up(i - 2)
        terms(i - 1)
        choose(i)

    add_up(count - 2)
    terms(count - 1)
    add_up(count - 1)

    moments(sums_ref[...], current_ref[:, owned:stations], normal_ref, right_ref, blocks, own_ref, other_ref)


def own_kernel(blocks, chunk, picks_ref, terms_ref, current_ref, normal_ref, right_ref, own_ref, other_ref):
    owned = own_ref.shape[1]
    sums = None
    for start in range(0, picks_ref.shape[1], chunk):
        more = station_sums(picks_ref, terms_ref, slice(0, owned), slice(start, start + chunk))
        sums = more if sums is None else sums + more
    moments(sums, current_ref[:, 0:owned], normal_ref, right_ref, blocks, own_ref, other_ref)


def own_moments(picks, terms, current, normal, right, owned, blocks):
    vmem = pl.BlockSpec(memory_space=pltpu.VMEM)
    return pl.pallas_call(
        partial(own_kernel, blocks, OWN_CHUNK),
        in_specs=[vmem] * 5,
        out_specs=[vmem] * 2,
        out_shape=[jax.ShapeDtypeStruct((11 * HALF, owned), F32)] * 2,
        compiler_params=pltpu.CompilerParams(vmem_limit_bytes=16 << 20),
        cost_estimate=pl.CostEstimate(
            flops=2 * owned * picks.shape[1] * terms.shape[0], transcendentals=0,
            bytes_accessed=2 * picks.shape[1] * (owned + terms.shape[0]),
        ),
        name="own_moments",
    )(picks, terms, current, normal, right)


def sweep(first, inputs, model, power, valid, visible, normal, right, owned, blocks):
    channels, baselines = valid.shape
    per = DIRECTIONS * channels
    count = owned * blocks
    vmem = pl.BlockSpec(memory_space=pltpu.VMEM)
    outs = [
        jax.ShapeDtypeStruct((11 * HALF, count - owned), F32),
        jax.ShapeDtypeStruct((11 * HALF, count - owned), F32),
        jax.ShapeDtypeStruct((2 * per, count), F32),
        jax.ShapeDtypeStruct((3 * per, 2 * baselines), BF16),
    ]
    if first:
        outs.append(jax.ShapeDtypeStruct((count, 2 * baselines), BF16))
    return pl.pallas_call(
        partial(sweep_kernel, first, blocks, owned, SWEEP_TILE),
        in_specs=[vmem] * (len(inputs) + 6),
        out_specs=[vmem] * len(outs),
        out_shape=outs,
        scratch_shapes=[
            pltpu.VMEM((2 * per, count), BF16),
            pltpu.VMEM((count - owned, 3 * per), F32),
            pltpu.VMEM((2 * per, 2 * SWEEP_TILE), F32),
            pltpu.VMEM((EXACT, 2 * SWEEP_TILE), BF16),
        ],
        compiler_params=pltpu.CompilerParams(vmem_limit_bytes=24 << 20),
        name="sweep",
    )(*inputs, model, power, valid, visible, normal, right)


def final_kernel(channels, before_ref, fit_ref, own_ref, other_ref, out_ref):
    per = DIRECTIONS * channels
    result = 0.5 * (before_ref[:, 0:out_ref.shape[3]] + fitted_values(fit_ref, own_ref, other_ref))
    for x in range(2):
        for d in range(DIRECTIONS):
            row = x * per + d * channels
            out_ref[x, d] = result[row:row + channels, :]


def finish(before, fit, own, other, channels):
    owned = own.shape[1]
    return pl.pallas_call(
        partial(final_kernel, channels),
        in_specs=[pl.BlockSpec(memory_space=pltpu.VMEM)] * 4,
        out_specs=pl.BlockSpec(memory_space=pltpu.VMEM),
        out_shape=jax.ShapeDtypeStruct((2, DIRECTIONS, channels, owned), F32),
        compiler_params=pltpu.CompilerParams(vmem_limit_bytes=8 << 20),
        name="finish",
    )(before, fit, own, other)


def solve(moments):
    m = [moments[k * HALF:(k + 1) * HALF] for k in range(11)]
    m.insert(3, 0.5 * (m[0] + m[2]))
    low_aa = jnp.sqrt(m[0])
    low_ba = m[1] / low_aa
    low_ca = m[2] / low_aa
    low_bb = jnp.sqrt(m[3] - low_ba * low_ba)
    low_cb = (m[4] - low_ca * low_ba) / low_bb
    low_cc = jnp.sqrt(m[5] - low_ca * low_ca - low_cb * low_cb)
    out = []
    for x in range(2):
        r = m[6 + 3 * x:9 + 3 * x]
        first_y = r[0] / low_aa
        second_y = (r[1] - low_ba * first_y) / low_bb
        third_y = (r[2] - low_ca * first_y - low_cb * second_y) / low_cc
        third_x = third_y / low_cc
        second_x = (second_y - low_cb * third_x) / low_bb
        first_x = (first_y - low_ba * second_x - low_ca * third_x) / low_aa
        out += [first_x, second_x, third_x]
    return jnp.concatenate(out, axis=0)


def other_core(value):
    count = lax.axis_size("chan")
    return lax.ppermute(value, "chan", [(j, j ^ 1) for j in range(count)])


def from_later(value, k, cross=False):
    count = lax.axis_size("bl")
    if not cross:
        return lax.ppermute(value, "bl", [((j + k) % count, j) for j in range(count)])
    pairs = [
        ((c ^ 1) * count + (j + k) % count, c * count + j) for c in range(lax.axis_size("chan")) for j in range(count)
    ]
    return lax.ppermute(value, ("chan", "bl"), pairs)


def over_chips(value):
    count = lax.axis_size("chan")
    chips = count // 2
    swap = lambda v, k: lax.ppermute(v, "chan", [(j, j ^ (2 * k)) for j in range(count)])
    if chips <= 4:
        order = (1, 3, 2) if chips == 4 else range(1, chips)
        parts = [swap(value, k) for k in order]
        for part in parts:
            value = value + part
        return value
    k = 1
    while k < chips:
        value = value + swap(value, k)
        k *= 2
    return value


def body(patches, visibilities, valid, baseline_stations, cluster, gains):
    channels = visibilities.shape[2]
    owned = gains.shape[3]
    blocks = lax.axis_size("bl")
    total = channels * lax.axis_size("chan")
    all_gains = [gains] + [from_later(gains, k) for k in range(1, blocks)]
    model, power, normal, right, fit = prepare(cluster[:, 0], patches, valid, total)
    common = (model, power, valid, visibilities, normal, right, owned, blocks)
    inputs = all_gains + [baseline_stations]
    picks = None
    for number in range(ITERS):
        own, other, current, terms, *made = sweep(number == 0, inputs, *common)
        picks = made[0] if made else picks
        others = own + other_core(other)
        others, terms = lax.optimization_barrier((others, terms))
        received = [
            from_later(others[:, (blocks - k - 1) * owned:(blocks - k) * owned], k) for k in range(1, blocks)
        ]
        own, other = own_moments(picks, terms, current, normal, right, owned, blocks)
        kept = own
        for part in received:
            kept = kept + part
        kept = lax.optimization_barrier(kept) + other_core(other)
        coefs = solve(over_chips(kept))
        if number < ITERS - 1:
            short = coefs.astype(BF16)
            across = [from_later(short, k, True).astype(F32) for k in range(1, blocks)]
            along = [from_later(short, k).astype(F32) for k in range(1, blocks)]
            beside = other_core(coefs)
            inputs = [current, fit, jnp.concatenate([coefs] + along, axis=1), jnp.concatenate([beside] + across, axis=1), picks]
        else:
            inputs = [current, fit, coefs, other_core(coefs), picks]
    return finish(*inputs[:4], channels)


def solution(mesh):
    in_specs = (
        P(None, None, None, ("grp", "chan"), "bl"),
        P(None, None, ("grp", "chan"), "bl"),
        P(("grp", "chan"), "bl"),
        P(None, "bl"),
        P(),
        P(None, None, ("grp", "chan"), "bl"),
    )
    out_specs = P(None, None, ("grp", "chan"), "bl")
    return jax.shard_map(body, mesh=mesh, in_specs=in_specs, out_specs=out_specs, check_vma=False)
```
